512 devices in a mesh: replica: 64 (over x, z), tensor: 8 (over y, core).
Axes of the slice: x: 4, y: 4, z: 16, core: 2. Of those that a mesh axis runs over, the one named last changes fastest.
Arguments:
- hidden: bfloat16 [4096, 8192], P('replica', 'tensor'), may hold values from -6 to 6
- base_query: bfloat16 [4096, 8192], P('replica', 'tensor'), may hold values from -6 to 6
- key_value_cache: bfloat16 [16384, 16, 2048], P('replica', None, 'tensor'), may hold values from -6 to 6
- adapter_down_weight: bfloat16 [1024, 16, 8192], P('replica', None, 'tensor'), may hold values from -0.0625 to 0.0625
- adapter_up_weight: bfloat16 [1024, 16, 8192], P('replica', None, 'tensor'), may hold values from -1.5 to 1.5
- adapter_holder: int32 [4096, 1], P('replica'), may hold values from 0 to 63; in each aligned block of 64 rows (0 to 63, 64 to 127, ...) at most 2 rows name the same one
- adapter_position: int32 [4096], P('replica'), may hold values from 0 to 15
- request_page_table: int32 [4096, 4], P('replica'), may hold values from 0 to 383, as said below
- lengths: int32 [4096], P('replica'), may hold values from 1 to 64, as said below
- migration_page_lists: int32 [64, 64, 2], P('replica'), may hold values from 0 to 255, as said below
Outputs:
- attended: bfloat16 [4096, 8192], P('replica', 'tensor')
The draws below stay inside these ranges and needn't reach their ends.
Inputs may be any that keep to these rules, and one draw needn't show every extreme that they name: `adapter_holder`: among the 64 requests of one device at most 2 name the same owner. Entries below 256 are distinct pages of the owner's own pool. A request with request_page_table[r, 0] of 256 or more has moved: all its entries are 256 + s * 2 + min(j, 1) for entry j, with one source s other than the owner; no two moved requests of one owner share a source. `lengths`: A moved request has at most 32 tokens. `migration_page_lists`: every entry of row s is a page of source s's pool; the pages that a moved request reads stand at entries 0 and 1 of the list of its source and owner.
All inputs are finite; a program needn't handle non-finite values.
Results may differ from the reference program's by a relative error of at most 0.011.
Values may be sent and summed in bfloat16 or wider, within the bound.
No kernel may reach another device: no remote copies, remote signals or barrier semaphores. Data moves between devices by JAX's collectives and lax.ppermute only.
A program may use at most 64 MiB of HBM per device.

```python
import math
import jax
import jax.numpy as jnp
import numpy as np
from jax import lax

MODEL_WIDTH = 8192
QUERY_HEADS = 64
KEY_VALUE_HEADS = 8
HEAD_SIZE = 128
ADAPTER_RANK = 16
ADP_DEV = 16
REQUEST_PER_COPY = 64
PAGE_TOKENS = 16
MAXP = 4
MIGP = 2
QCAP = 1
ACAP = 2
MOVED = 32
MIGCAP = 2
POOL_PAGES = 256
REQUEST_TOTAL = 4096
ADAPTER_TOTAL = 1024
N_REPLICA = 64


def layout(key):
    device_count = N_REPLICA
    key_cycle, key_slots, key_place, key_shift, key_len, key_moved = jax.random.split(key, 6)
    order = jax.random.permutation(key_cycle, device_count).astype(jnp.int32)
    where_in = jnp.zeros((device_count,), jnp.int32).at[order].set(jnp.arange(device_count, dtype=jnp.int32))
    devices = jnp.arange(device_count, dtype=jnp.int32)
    chosen = jax.vmap(lambda device: jax.random.permutation(jax.random.fold_in(key_slots, device), REQUEST_PER_COPY))(devices).astype(jnp.int32)
    place = jax.vmap(lambda device: jax.random.permutation(jax.random.fold_in(key_place, device), POOL_PAGES))(devices).astype(jnp.int32)
    steps_in = jnp.arange(MIGP, dtype=jnp.int32)
    mig = jnp.broadcast_to(place[:, None, :MIGCAP], (device_count, device_count, MIGCAP))
    table = place.reshape(device_count, REQUEST_PER_COPY, MAXP)
    capped = jnp.minimum(jnp.arange(MAXP, dtype=jnp.int32), MIGP - 1)[None, :]
    shift = jax.random.randint(key_shift, (device_count, REQUEST_PER_COPY), 0, 4)
    top_len = jnp.right_shift(jnp.int32(MAXP * PAGE_TOKENS), shift.astype(jnp.int32))
    lens = jax.random.randint(key_len, (device_count, REQUEST_PER_COPY), 1, top_len + 1).astype(jnp.int32)
    moved_len = jax.random.randint(key_moved, (device_count, MOVED), PAGE_TOKENS + 1, MIGP * PAGE_TOKENS + 1).astype(jnp.int32)
    for step in range(MOVED):
        succ = order[(where_in + step + 1) % device_count]
        pred = order[(where_in - step - 1) % device_count]
        pages = place[devices[:, None], chosen[:, step:step + 1] * MAXP + steps_in[None, :]]
        mig = mig.at[devices, succ].set(pages)
        table = table.at[devices, chosen[:, step]].set(POOL_PAGES + pred[:, None] * MIGCAP + capped)
        lens = lens.at[devices, chosen[:, step]].set(moved_len[:, step])
    lens = lens.at[0, chosen[0, MOVED]].set(MAXP * PAGE_TOKENS)
    lens = lens.at[0, chosen[0, 0]].set(MIGP * PAGE_TOKENS)
    return (table.reshape(device_count * REQUEST_PER_COPY, MAXP), lens.reshape(device_count * REQUEST_PER_COPY), mig)


def draw_request_page_table(key, part):
    shared = layout(key)
    return shared[0]


def draw_lengths(key, part):
    shared = layout(key)
    return shared[1]


def draw_migration_page_lists(key, part):
    shared = layout(key)
    return shared[2]


def draw_base_query(key, part):
    key = jax.random.fold_in(key, 11)
    key_base = jax.random.fold_in(key, 0)
    values = jnp.clip(jax.random.normal(key_base, (REQUEST_TOTAL, QUERY_HEADS * HEAD_SIZE), jnp.float32), -6.0, 6.0)
    return values.astype(jnp.bfloat16)


def draw_key_value_cache(key, part):
    key = jax.random.fold_in(key, 12)
    full_shape = (N_REPLICA * POOL_PAGES, PAGE_TOKENS, KEY_VALUE_HEADS * 2 * HEAD_SIZE)
    values = jnp.clip(jax.random.normal(key, full_shape, jnp.float32), -6.0, 6.0)
    return values.astype(jnp.bfloat16)


def set_ends(entries, own_key, smallest, high):
    longest = entries.shape.index(max(entries.shape))
    spots = []
    for shift in (0, 1):
        where = [jax.random.randint(jax.random.fold_in(own_key, axis), (), 0, length) for axis, length in enumerate(entries.shape)]
        where[longest] = (where[longest] + shift) % entries.shape[longest]
        spots.append(tuple(where))
    return entries.at[spots[0]].set(smallest).at[spots[1]].set(high)


def level_of(rng, dims, cuts, smallest, largest):
    factor_of, own = 1.0, jax.random.fold_in(rng, 6)
    for dim, parts in cuts:
        steps = jnp.exp(jax.random.uniform(jax.random.fold_in(own, dim), (parts,), jnp.float32, smallest / len(cuts), largest / len(cuts)))
        factor_of = factor_of * jnp.repeat(steps, dims[dim] // parts).reshape([-1 if axis == dim else 1 for axis in range(len(dims))])
    return factor_of


def routed_block(rng, own, number, rows, count, top, bound, slope):
    sequence = jax.random.permutation(rng, count)
    packed, ordinary = shares(count, rows * top, bound, slope, True), shares(count, rows * top, bound, slope, False)
    places = jnp.arange(count)

    def named(sizes, rotation):
        used = int((sizes > 0).sum())
        fixed = max(1, used // 4)
        shifted = fixed + (places - fixed + rotation * (used - fixed)) % max(1, count - fixed)
        return jnp.zeros((count,), jnp.int32).at[sequence[jnp.where(places < fixed, places, shifted)]].set(jnp.asarray(sizes, jnp.int32))

    sizes = jnp.where(number % 4 == 0, named(packed, number // 4), named(ordinary, number - number // 4 - 1))
    mixed = jax.random.permutation(jax.random.fold_in(own, 3), count)
    giver, receiver = mixed[0:count // 2 * 2:2], mixed[1:count // 2 * 2:2]
    margin = jnp.minimum(sizes[giver] - 1, bound - sizes[receiver]) // 2
    margin = jnp.where((giver == sequence[0]) | (receiver == sequence[0]) | (sizes[receiver] == 0), 0, jnp.maximum(margin, 0))
    shifted = jax.random.randint(jax.random.fold_in(own, 4), (count // 2,), 0, 1 << 20) % (margin + 1)
    sizes = sizes.at[giver].add(-shifted).at[receiver].add(shifted)
    labels = jnp.searchsorted(jnp.cumsum(sizes), jnp.arange(rows * top), side="right").astype(jnp.int32)
    grid = labels.reshape(top, rows).T
    grid = grid[jax.random.permutation(jax.random.fold_in(own, 1), rows)]
    rotation = jax.random.randint(jax.random.fold_in(own, 2), (rows, 1), 0, top)
    return jnp.take_along_axis(grid, (jnp.arange(top)[None, :] + rotation) % top, axis=1)


def shares(count, total, reach, skew, full):
    loads = [(1 << 20) // math.isqrt(rank ** skew) + 1 for rank in range(1, count + 1)]
    largest = reach if full else min(reach, max(-(-total // count), total * loads[0] // sum(loads)))
    least = 1 if total - largest >= count - 1 else 0
    counts, spare = [largest] + [least] * (count - 1), total - largest - least * (count - 1)
    while spare > 0:
        candidates = [i for i in range(1, count) if counts[i] < largest] or [i for i in range(1, count) if counts[i] < reach]
        pool, remaining = sum([loads[i] for i in candidates]), spare
        for i in candidates:
            extra = min(reach - counts[i], max(1, remaining * loads[i] // pool), spare)
            counts[i] = counts[i] + extra
            spare = spare - extra
    return np.array(counts)


def gaussian(own_key, extent, width, most, shards=(), kind=jnp.bfloat16):
    entries = jax.random.normal(own_key, extent, jnp.float32) * width
    if len(shards) > 0:
        entries = level_of(own_key, extent, shards, -0.22, 0.18) * entries
    return jnp.clip(entries, min=-most, max=most).astype(kind)


def setup_inputs(seed: int = 0) -> dict:
    streams_of = jax.random.split(jax.random.key(seed), 11)
    hidden = gaussian(streams_of[0], (REQUEST_TOTAL, MODEL_WIDTH), 1.0, 6.0, ((0, 64), (1, 8)))
    base_query = draw_base_query(jax.random.fold_in(streams_of[10], 71), 0)
    key_value_cache = draw_key_value_cache(jax.random.fold_in(streams_of[10], 71), 0)
    adapter_down_weight = gaussian(streams_of[3], (ADAPTER_TOTAL, ADAPTER_RANK, MODEL_WIDTH), MODEL_WIDTH ** -0.5, 0.0625, ((0, 64), (2, 8)))
    adapter_up_weight = gaussian(streams_of[4], (ADAPTER_TOTAL, ADAPTER_RANK, MODEL_WIDTH), ADAPTER_RANK ** -0.5, 1.5, ((0, 64), (2, 8)))
    adapter_holder_keys = jax.random.split(jax.random.fold_in(streams_of[5], 1), REQUEST_TOTAL // REQUEST_PER_COPY)
    adapter_holder_turns = jax.random.permutation(jax.random.fold_in(streams_of[5], 3), REQUEST_TOTAL // REQUEST_PER_COPY)
    adapter_holder = jax.vmap(lambda own, number: routed_block(jax.random.fold_in(streams_of[5], 2), own, number, REQUEST_PER_COPY, N_REPLICA, 1, ACAP, 2))(adapter_holder_keys, adapter_holder_turns).reshape((REQUEST_TOTAL, 1))
    adapter_position = set_ends(jax.random.randint(streams_of[6], (REQUEST_TOTAL,), 0, ADP_DEV), jax.random.fold_in(streams_of[6], 1), 0, ADP_DEV - 1).astype(jnp.int32)
    request_page_table = draw_request_page_table(jax.random.fold_in(streams_of[10], 71), 0)
    lengths = draw_lengths(jax.random.fold_in(streams_of[10], 71), 0)
    migration_page_lists = draw_migration_page_lists(jax.random.fold_in(streams_of[10], 71), 0)
    return dict(hidden=hidden, base_query=base_query, key_value_cache=key_value_cache, adapter_down_weight=adapter_down_weight, adapter_up_weight=adapter_up_weight, adapter_holder=adapter_holder, adapter_position=adapter_position, request_page_table=request_page_table, lengths=lengths, migration_page_lists=migration_page_lists)


adapter_scale = 2.0


def attend(query_rows, page_rows, valid_len):
    row_count = query_rows.shape[0]
    key_count = page_rows.shape[1]
    kv_heads = page_rows.shape[2] // (2 * HEAD_SIZE)
    grouped = query_rows.reshape(row_count, kv_heads, -1, HEAD_SIZE).astype(jnp.float32)
    stacked = page_rows.reshape(row_count, key_count, kv_heads, 2, HEAD_SIZE).astype(jnp.float32)
    scores = jnp.einsum("rhge,rlhe->rhgl", grouped, stacked[:, :, :, 0]) * (HEAD_SIZE ** -0.5)
    live_mask = (jnp.arange(key_count, dtype=jnp.int32)[None, :] < valid_len[:, None])[:, None, None, :]
    scores = jnp.where(live_mask, scores, -jnp.inf)
    row_max = jnp.max(scores, axis=-1, keepdims=True)
    weights = jnp.exp(scores - row_max)
    row_total = jnp.sum(weights, axis=-1, keepdims=True)
    weights_bf = (weights / row_total).astype(jnp.bfloat16)
    mixed = jnp.einsum("rhgl,rlhe->rhge", weights_bf.astype(jnp.float32), stacked[:, :, :, 1])
    return mixed.reshape(row_count, -1).astype(jnp.bfloat16)


def reference(hidden, base_query, key_value_cache, adapter_down_weight, adapter_up_weight, adapter_holder, adapter_position, request_page_table, lengths, migration_page_lists):
    adapter_numbers = adapter_holder[:, 0] * ADP_DEV + adapter_position

    def adapter_block(pair_entry):
        block_row_set, block_numbers = pair_entry
        down_weight_rows = adapter_down_weight[block_numbers].astype(jnp.float32)
        reduced_rank_state = jnp.einsum("jq,jhq->jh", block_row_set.astype(jnp.float32), down_weight_rows).astype(jnp.bfloat16)
        up_weight_rows = adapter_up_weight[block_numbers].astype(jnp.float32)
        return (jnp.einsum("vr,vrt->vt", reduced_rank_state.astype(jnp.float32), up_weight_rows) * adapter_scale).astype(jnp.bfloat16)

    adapter_delta = lax.map(adapter_block, (hidden.reshape(N_REPLICA, REQUEST_PER_COPY, MODEL_WIDTH), adapter_numbers.reshape(N_REPLICA, REQUEST_PER_COPY)))
    adapter_delta = adapter_delta.reshape(REQUEST_TOTAL, MODEL_WIDTH)
    query_matrix = (base_query.astype(jnp.float32) + adapter_delta.astype(jnp.float32)).astype(jnp.bfloat16)
    owner_dev = (jnp.arange(REQUEST_TOTAL, dtype=jnp.int32) // REQUEST_PER_COPY)[:, None]
    migrated = request_page_table >= POOL_PAGES
    offset = jnp.maximum(request_page_table - POOL_PAGES, 0)
    source_dev = offset // MIGCAP
    move_rank = jnp.minimum((offset % MIGCAP) // MIGP, QCAP - 1)
    list_slot = move_rank * MIGP + offset % MIGP
    global_page = jnp.where(migrated, source_dev * POOL_PAGES + migration_page_lists[source_dev, owner_dev, list_slot], owner_dev * POOL_PAGES + request_page_table)

    def attend_block(triple):
        block_q, block_pages, block_len = triple
        page_rows = key_value_cache[block_pages].reshape(REQUEST_PER_COPY, MAXP * PAGE_TOKENS, -1)
        return attend(block_q, page_rows, block_len)

    attended = lax.map(attend_block, (query_matrix.reshape(N_REPLICA, REQUEST_PER_COPY, QUERY_HEADS * HEAD_SIZE), global_page.reshape(N_REPLICA, REQUEST_PER_COPY, MAXP), lengths.reshape(N_REPLICA, REQUEST_PER_COPY)))
    return attended.reshape(REQUEST_TOTAL, QUERY_HEADS * HEAD_SIZE)
```

```python
import jax
import jax.numpy as jnp
from jax import lax
from jax.experimental import pallas as pl
from jax.experimental.pallas import tpu as pltpu
from jax.sharding import PartitionSpec as P

HEAD = 128
RANK = 16
PAGE = 16
POOL = 256
SCALE = 2.0
F32 = jnp.float32
BF16 = jnp.bfloat16
NEG = -1e30


def dot(a, b, dims):
    return lax.dot_general(a, b, (dims, ((), ())), preferred_element_type=F32)


def nn(a, b):
    return dot(a, b, ((1,), (0,)))


def nt(a, b):
    return dot(a, b, ((1,), (1,)))


def tn(a, b):
    return dot(a, b, ((0,), (0,)))


def iota(shape, dim):
    return lax.broadcasted_iota(jnp.int32, shape, dim)


def slot_maps(holder_row, peers):
    rows = holder_row.shape[1]
    named = iota((peers, rows), 0) == holder_row
    before = (iota((rows, rows), 0) < iota((rows, rows), 1)).astype(BF16)
    rank = nn(named.astype(BF16), before)
    return [(named & (rank == c)).astype(BF16) for c in range(2)]


def moved_map(table, peers):
    entry = table[0:1, :]
    source = lax.shift_right_arithmetic(entry - POOL, 1)
    return (iota((peers, entry.shape[1]), 0) == source) & (entry >= POOL)


def send_kernel(hidden_ref, holder_ref, position_ref, table_ref, lengths_ref, out_ref):
    peers, _, width = out_ref.shape
    features = width - HEAD
    maps = slot_maps(holder_ref[...], peers)
    hidden = hidden_ref[...]
    rows = hidden.shape[0]
    place = (iota((HEAD, rows), 0) == position_ref[...]).astype(BF16)
    moved = moved_map(table_ref[...], peers)
    length = jnp.sum(jnp.where(moved, lengths_ref[...], 0).astype(F32), axis=1, keepdims=True)
    lane = iota((peers, HEAD), 1)
    for c in range(2):
        out_ref[:, c, :features] = nn(maps[c], hidden).astype(BF16)
        out_ref[:, c, features:] = jnp.where(lane < RANK, nt(maps[c], place), length).astype(BF16)


def down_kernel(got_ref, down_ref, partial_ref, pick_ref, limit_ref):
    peers, _, width = got_ref.shape
    features = width - HEAD
    down = down_ref[...]
    many = down.shape[0]
    first, second = got_ref[:, 0, :], got_ref[:, 1, :]
    got = jnp.concatenate([first[:, :features], second[:, :features]], axis=0)
    place = jnp.concatenate([first[:, features:], second[:, features:]], axis=0)
    spread = (lax.shift_right_arithmetic(iota((many, HEAD), 0), 4) == iota((many, HEAD), 1)).astype(BF16)
    pick = nt(spread, place)
    projected = nt(down, got) * pick
    partial = jnp.sum(projected.reshape(many // RANK, RANK, 2 * peers), axis=0)
    for t in range(partial_ref.shape[0]):
        partial_ref[t] = partial
    pick_ref[...] = pick.astype(BF16)
    tail = first[:, features:].astype(F32)
    limit_ref[...] = jnp.broadcast_to(tail[:, None, :], limit_ref.shape)


def up_kernel(got_ref, pick_ref, up_ref, out_ref):
    peers = out_ref.shape[0]
    low = jnp.sum(got_ref[...], axis=0).astype(BF16)
    many = up_ref.shape[0]
    spread = jnp.concatenate([low] * (many // RANK), axis=0) * pick_ref[...]
    delta = (tn(spread, up_ref[...]) * SCALE).astype(BF16)
    for c in range(2):
        out_ref[:, c, :] = delta[c * peers:(c + 1) * peers, :]


def query_kernel(got_ref, base_ref, holder_ref, table_ref, query_ref, out_ref, wide_ref):
    peers = got_ref.shape[0]
    maps = slot_maps(holder_ref[...], peers)
    delta = tn(maps[0], got_ref[:, 0, :]) + tn(maps[1], got_ref[:, 1, :])
    query = (base_ref[...].astype(F32) + delta).astype(BF16)
    query_ref[...] = query
    moved = moved_map(table_ref[...], peers).astype(BF16)
    chosen = nn(moved, query)
    heads = wide_ref.shape[1]
    for h in range(heads):
        wide_ref[:, h, :] = chosen[:, h * HEAD:(h + 1) * HEAD]
    out_ref[...] = wide_ref[...].astype(BF16)


def weighted(scores, live, values):
    scores = jnp.where(live, scores * (HEAD ** -0.5), NEG)
    top = jnp.max(scores, axis=1, keepdims=True)
    weights = jnp.exp(scores - top)
    total = jnp.sum(weights, axis=1, keepdims=True)
    return nn((weights / total).astype(BF16), values)


def local_kernel(table_ref, lengths_ref, query_ref, cache_ref, row_ref, out_ref, wide_ref, mixed_ref):
    rows, heads, _ = wide_ref.shape
    pages = table_ref.shape[0]
    span = pages * PAGE
    query = query_ref[...]
    for h in range(heads):
        wide_ref[:, h, :] = query[:, h * HEAD:(h + 1) * HEAD].astype(F32)
    batch = 4
    shape = (batch * heads, batch * span)
    row_of = lax.div(iota(shape, 0), heads)
    column_of = lax.div(iota(shape, 1), span)
    place = lax.rem(iota(shape, 1), span)
    own = row_of == column_of

    def step(b, carry):
        first = b * batch
        found = []
        limit = jnp.zeros(shape, jnp.int32)
        for i in range(batch):
            limit = jnp.where(row_of == i, lengths_ref[0, first + i], limit)
            for j in range(pages):
                found.append(cache_ref[jnp.minimum(table_ref[j, first + i], POOL - 1)])
        both = jnp.concatenate(found, axis=0)
        q = wide_ref[pl.ds(first, batch)].reshape(batch * heads, HEAD).astype(BF16)
        scores = nt(q, both[:, :HEAD])
        mixed = weighted(scores, own & (place < limit), both[:, HEAD:])
        mixed_ref[pl.ds(first, batch)] = mixed.reshape(batch, heads, HEAD)
        return carry

    lax.fori_loop(0, rows // batch, step, 0, unroll=4)
    stays = jnp.where(row_ref[0:1, :] < POOL, 1.0, 0.0)
    eye = iota((rows, rows), 0) == iota((rows, rows), 1)
    keep = jnp.sum(jnp.where(eye, stays, 0.0), axis=1, keepdims=True)
    for h in range(heads):
        out_ref[:, h * HEAD:(h + 1) * HEAD] = (mixed_ref[:, h, :] * keep).astype(BF16)


def listed_kernel(list_ref, cache_ref, key_ref, value_ref):
    count, owners = list_ref.shape

    def step(o, carry):
        for k in range(count):
            page = cache_ref[list_ref[k, o]]
            at = pl.ds(pl.multiple_of((o * count + k) * PAGE, PAGE), PAGE)
            key_ref[at, :] = page[:, :HEAD]
            value_ref[at, :] = page[:, HEAD:]
        return carry

    lax.fori_loop(0, owners, step, 0, unroll=8)


def moved_kernel(query_ref, key_ref, value_ref, limit_ref, out_ref):
    owners, heads, _ = query_ref.shape
    span = key_ref.shape[0] // owners
    batch = 8
    shape = (batch * heads, batch * span)
    own = lax.div(iota(shape, 0), heads) == lax.div(iota(shape, 1), span)
    place = lax.rem(iota(shape, 1), span)
    for b in range(owners // batch):
        at = slice(b * batch, (b + 1) * batch)
        keys = slice(b * batch * span, (b + 1) * batch * span)
        q = query_ref[at].astype(F32).reshape(batch * heads, HEAD).astype(BF16)
        limit = limit_ref[at].reshape(batch * heads, HEAD)[:, HEAD - 1:HEAD]
        live = own & (place.astype(F32) < limit)
        mixed = weighted(nt(q, key_ref[keys, :]), live, value_ref[keys, :])
        out_ref[at] = mixed.reshape(batch, heads, HEAD).astype(BF16)


def final_kernel(got_ref, local_ref, table_ref, out_ref, wide_ref):
    peers, heads, _ = got_ref.shape
    wide_ref[...] = got_ref[...].astype(F32)
    moved = moved_map(table_ref[...], peers).astype(BF16)
    for h in range(heads):
        part = tn(moved, wide_ref[:, h, :].astype(BF16))
        at = slice(h * HEAD, (h + 1) * HEAD)
        out_ref[:, at] = (part + local_ref[:, at].astype(F32)).astype(BF16)


def call(kernel, out_shape, cost, scratch=(), scalars=0, inputs=0):
    smem = pl.BlockSpec(memory_space=pltpu.SMEM)
    vmem = pl.BlockSpec(memory_space=pltpu.VMEM)
    return pl.pallas_call(
        kernel,
        out_shape=out_shape,
        in_specs=[smem] * scalars + [vmem] * inputs,
        out_specs=jax.tree.map(lambda _: vmem, out_shape),
        scratch_shapes=list(scratch),
        cost_estimate=pl.CostEstimate(flops=cost, bytes_accessed=cost // 100, transcendentals=0),
        compiler_params=pltpu.CompilerParams(vmem_limit_bytes=24 * 1024 * 1024),
    )


def exchange(x, axis="replica"):
    return lax.all_to_all(x, axis, split_axis=0, concat_axis=0, tiled=True)


def body(
    hidden,
    base_query,
    key_value_cache,
    adapter_down_weight,
    adapter_up_weight,
    adapter_holder,
    adapter_position,
    request_page_table,
    lengths,
    migration_page_lists,
):
    rows, features = hidden.shape
    peers = lax.axis_size("replica")
    shards = lax.axis_size("tensor")
    heads = features // HEAD
    S = jax.ShapeDtypeStruct
    holder = adapter_holder.reshape(1, rows)
    position = adapter_position.reshape(1, rows)
    table = request_page_table.T
    length = lengths.reshape(1, rows)
    lists = migration_page_lists[0].T
    down = adapter_down_weight.reshape(-1, features)
    up = adapter_up_weight.reshape(-1, features)
    many = down.shape[0]

    sent = call(send_kernel, S((peers, 2, features + HEAD), BF16), 10**8, inputs=5)(
        hidden, holder, position, table, length
    )
    got = exchange(sent)
    span = lists.shape[0] * PAGE
    keys, values = call(
        listed_kernel, (S((peers * span, HEAD), BF16),) * 2, 10**9, scalars=1, inputs=1
    )(lists, key_value_cache)

    partial, pick, limit = call(
        down_kernel,
        (S((shards, RANK, 2 * peers), F32), S((many, 2 * peers), BF16), S((peers, heads, HEAD), F32)),
        10**8,
        inputs=2,
    )(got, down)
    partials = exchange(partial, "tensor")
    delta = call(up_kernel, S((peers, 2, features), BF16), 10**8, inputs=3)(partials, pick, up)
    returned = exchange(delta)
    wide = pltpu.VMEM((rows, heads, HEAD), F32)
    query, moved_query = call(
        query_kernel, (S((rows, features), BF16), S((peers, heads, HEAD), BF16)), 10**8, (wide,), inputs=4
    )(returned, base_query, holder, table)
    asked = exchange(moved_query)
    local = call(local_kernel, S((rows, features), BF16), 10**9, (wide, wide), scalars=2, inputs=3)(
        table, length, query, key_value_cache, table
    )
    answer = call(moved_kernel, S((peers, heads, HEAD), BF16), 10**8, inputs=4)(asked, keys, values, limit)
    answered = exchange(answer)
    return call(final_kernel, S((rows, features), BF16), 10**8, (wide,), inputs=3)(answered, local, table)


def solution(mesh):
    in_specs = (
        P("replica", "tensor"),
        P("replica", "tensor"),
        P("replica", None, "tensor"),
        P("replica", None, "tensor"),
        P("replica", None, "tensor"),
        P("replica", None),
        P("replica"),
        P("replica", None),
        P("replica"),
        P("replica", None, None),
    )
    return jax.shard_map(body, mesh=mesh, in_specs=in_specs, out_specs=P("replica", "tensor"), check_vma=False)
```

```python
import jax
import jax.numpy as jnp
from jax import lax
from jax.experimental import pallas as pl
from jax.experimental.pallas import tpu as pltpu
from jax.sharding import PartitionSpec as P

HEAD = 128
RANK = 16
PAGE = 16
POOL = 256
SCALE = 2.0
F32 = jnp.float32
BF16 = jnp.bfloat16
NEG = -1e30


def dot(a, b, dims):
    return lax.dot_general(a, b, (dims, ((), ())), preferred_element_type=F32)


def nn(a, b):
    return dot(a, b, ((1,), (0,)))


def nt(a, b):
    return dot(a, b, ((1,), (1,)))


def tn(a, b):
    return dot(a, b, ((0,), (0,)))


def iota(shape, dim):
    return lax.broadcasted_iota(jnp.int32, shape, dim)


def slot_maps(holder_row, peers):
    rows = holder_row.shape[1]
    named = iota((peers, rows), 0) == holder_row
    before = (iota((rows, rows), 0) < iota((rows, rows), 1)).astype(BF16)
    rank = nn(named.astype(BF16), before)
    return [(named & (rank == c)).astype(BF16) for c in range(2)]


def moved_map(table, peers):
    entry = table[0:1, :]
    source = lax.shift_right_arithmetic(entry - POOL, 1)
    return (iota((peers, entry.shape[1]), 0) == source) & (entry >= POOL)


def fetch(pairs, sems):
    copies = [pltpu.make_async_copy(src, dst, sems.at[i]) for i, (src, dst) in enumerate(pairs)]
    for copy in copies:
        copy.start()
    return copies


def send_kernel(
    hidden_hbm, holder_hbm, position_hbm, table_hbm, lengths_hbm, out_ref,
    hidden_ref, holder_ref, position_ref, table_ref, lengths_ref, sems,
):
    peers, _, width = out_ref.shape
    features = width - HEAD
    copies = fetch(
        [
            (holder_hbm, holder_ref),
            (position_hbm, position_ref),
            (table_hbm, table_ref),
            (lengths_hbm, lengths_ref),
            (hidden_hbm, hidden_ref),
        ],
        sems,
    )
    for copy in copies[:4]:
        copy.wait()
    maps = slot_maps(holder_ref[...], peers)
    rows = hidden_ref.shape[0]
    place = (iota((HEAD, rows), 0) == position_ref[...]).astype(BF16)
    moved = moved_map(table_ref[...], peers)
    length = jnp.sum(jnp.where(moved, lengths_ref[...], 0).astype(F32), axis=1, keepdims=True)
    lane = iota((peers, HEAD), 1)
    for c in range(2):
        out_ref[:, c, features:] = jnp.where(lane < RANK, nt(maps[c], place), length).astype(BF16)
    copies[4].wait()
    hidden = hidden_ref[...]
    for c in range(2):
        out_ref[:, c, :features] = nn(maps[c], hidden).astype(BF16)


def down_kernel(got_ref, down_ref, partial_ref, pick_ref, limit_ref):
    peers, _, width = got_ref.shape
    features = width - HEAD
    many = down_ref.shape[0]
    first, second = got_ref[:, 0, :], got_ref[:, 1, :]
    got = jnp.concatenate([first[:, :features], second[:, :features]], axis=0)
    place = jnp.concatenate([first[:, features:], second[:, features:]], axis=0)
    spread = (lax.shift_right_arithmetic(iota((many, HEAD), 0), 4) == iota((many, HEAD), 1)).astype(BF16)
    pick = nt(spread, place)
    pick_ref[...] = pick.astype(BF16)
    tail = first[:, width - 1:].astype(F32)
    limit_ref[...] = jnp.broadcast_to(tail[:, None, :], limit_ref.shape)
    projected = nt(down_ref[...], got) * pick
    partial = jnp.sum(projected.reshape(many // RANK, RANK, 2 * peers), axis=0)
    for t in range(partial_ref.shape[0]):
        partial_ref[t] = partial


def up_kernel(got_ref, pick_ref, up_ref, out_ref):
    peers = out_ref.shape[0]
    low = jnp.sum(got_ref[...], axis=0).astype(BF16)
    many = up_ref.shape[0]
    spread = jnp.concatenate([low] * (many // RANK), axis=0) * pick_ref[...]
    delta = (tn(spread, up_ref[...]) * SCALE).astype(BF16)
    for c in range(2):
        out_ref[:, c, :] = delta[c * peers:(c + 1) * peers, :]


def prepare_kernel(
    list_ref, cache_ref, holder_ref, table_ref, base_ref, weight_ref, page_ref, route_ref, start_ref, down_ref
):
    down_ref[...] = weight_ref[...]
    count, owners = list_ref.shape

    def step(o, carry):
        for k in range(count):
            at = pl.ds(pl.multiple_of((o * count + k) * PAGE, PAGE), PAGE)
            page_ref[at, :] = cache_ref[list_ref[k, o]]
        return carry

    lax.fori_loop(0, owners, step, 0, unroll=8)
    maps = slot_maps(holder_ref[...], owners)
    moved = moved_map(table_ref[...], owners).astype(BF16)
    route_ref[...] = nt(jnp.concatenate(maps, axis=0), moved).astype(BF16)
    start = nn(moved, base_ref[...])
    for h in range(start_ref.shape[1]):
        start_ref[:, h, :] = start[:, h * HEAD:(h + 1) * HEAD]


def query_kernel(got_ref, route_ref, start_ref, out_ref, wide_ref):
    got = jnp.concatenate([got_ref[:, 0, :], got_ref[:, 1, :]], axis=0)
    chosen = tn(route_ref[...], got)
    for h in range(wide_ref.shape[1]):
        wide_ref[:, h, :] = chosen[:, h * HEAD:(h + 1) * HEAD]
    out_ref[...] = (start_ref[...] + wide_ref[...]).astype(BF16)


def weighted(scores, live, values):
    scores = jnp.where(live, scores * (HEAD ** -0.5), NEG)
    top = jnp.max(scores, axis=1, keepdims=True)
    weights = jnp.exp(scores - top)
    total = jnp.sum(weights, axis=1, keepdims=True)
    return nn((weights / total).astype(BF16), values)


def local_kernel(
    table_ref, lengths_ref, got_ref, base_ref, holder_ref, row_ref, cache_ref, out_ref, wide_ref, mixed_ref
):
    rows, heads, _ = wide_ref.shape
    pages = table_ref.shape[0]
    span = pages * PAGE
    maps = jnp.concatenate(slot_maps(holder_ref[...], got_ref.shape[0]), axis=0)
    delta = tn(maps, jnp.concatenate([got_ref[:, 0, :], got_ref[:, 1, :]], axis=0))
    query = (base_ref[...].astype(F32) + delta).astype(BF16).astype(F32)
    for h in range(heads):
        wide_ref[:, h, :] = query[:, h * HEAD:(h + 1) * HEAD]
    batch = 4
    shape = (batch * heads, batch * span)
    row_of = lax.div(iota(shape, 0), heads)
    column_of = lax.div(iota(shape, 1), span)
    place = lax.rem(iota(shape, 1), span)
    own = row_of == column_of

    def step(b, carry):
        first = b * batch
        found = []
        limit = jnp.zeros(shape, jnp.int32)
        for i in range(batch):
            limit = jnp.where(row_of == i, lengths_ref[0, first + i], limit)
            for j in range(pages):
                found.append(cache_ref[jnp.minimum(table_ref[j, first + i], POOL - 1)])
        both = jnp.concatenate(found, axis=0)
        q = wide_ref[pl.ds(first, batch)].reshape(batch * heads, HEAD).astype(BF16)
        scores = nt(q, both[:, :HEAD])
        mixed = weighted(scores, own & (place < limit), both[:, HEAD:])
        mixed_ref[pl.ds(first, batch)] = mixed.reshape(batch, heads, HEAD)
        return carry

    lax.fori_loop(0, rows // batch, step, 0, unroll=4)
    stays = jnp.where(row_ref[0:1, :] < POOL, 1.0, 0.0)
    eye = iota((rows, rows), 0) == iota((rows, rows), 1)
    keep = jnp.sum(jnp.where(eye, stays, 0.0), axis=1, keepdims=True)
    for h in range(heads):
        out_ref[:, h * HEAD:(h + 1) * HEAD] = (mixed_ref[:, h, :] * keep).astype(BF16)


def moved_kernel(query_ref, page_ref, limit_ref, out_ref):
    owners, heads, _ = query_ref.shape
    span = page_ref.shape[0] // owners
    batch = HEAD // span
    groups = owners // batch
    wide = batch * heads
    shape = (wide, batch * span)
    own = lax.div(iota(shape, 0), heads) == lax.div(iota(shape, 1), span)
    place = jnp.where(own, lax.rem(iota(shape, 1), span), span).astype(F32)
    query = query_ref[...].astype(F32).reshape(owners * heads, HEAD).astype(BF16)
    pages = [page_ref[g * HEAD:(g + 1) * HEAD, :] for g in range(groups)]
    scores = [nt(query[g * wide:(g + 1) * wide], pages[g][:, :HEAD]) for g in range(groups)]
    live = [
        place < limit_ref[g * batch:(g + 1) * batch].reshape(wide, HEAD) for g in range(groups)
    ]
    scores = [jnp.where(m, x * (HEAD ** -0.5), NEG) for m, x in zip(live, scores)]
    tops = [jnp.max(x, axis=1, keepdims=True) for x in scores]
    weights = [jnp.exp(x - top) for x, top in zip(scores, tops)]
    totals = [jnp.sum(x, axis=1, keepdims=True) for x in weights]
    weights = [(x / total).astype(BF16) for x, total in zip(weights, totals)]
    mixed = [nn(x, page[:, HEAD:]) for x, page in zip(weights, pages)]
    for g in range(groups):
        out_ref[g * batch:(g + 1) * batch] = mixed[g].reshape(batch, heads, HEAD).astype(BF16)


def final_kernel(got_ref, local_ref, table_ref, out_ref, wide_ref):
    peers, heads, _ = got_ref.shape
    wide_ref[...] = got_ref[...].astype(F32)
    moved = moved_map(table_ref[...], peers).astype(BF16)
    for h in range(heads):
        part = tn(moved, wide_ref[:, h, :].astype(BF16))
        at = slice(h * HEAD, (h + 1) * HEAD)
        out_ref[:, at] = (part + local_ref[:, at].astype(F32)).astype(BF16)


def call(kernel, out_shape, cost, spaces, scratch=(), limit=24):
    kinds = {"s": pltpu.SMEM, "v": pltpu.VMEM, "h": pltpu.HBM}
    return pl.pallas_call(
        kernel,
        out_shape=out_shape,
        in_specs=[pl.BlockSpec(memory_space=kinds[x]) for x in spaces],
        out_specs=jax.tree.map(lambda _: pl.BlockSpec(memory_space=pltpu.VMEM), out_shape),
        scratch_shapes=list(scratch),
        cost_estimate=pl.CostEstimate(flops=cost, bytes_accessed=cost // 100, transcendentals=0),
        compiler_params=pltpu.CompilerParams(vmem_limit_bytes=limit * 1024 * 1024),
    )


def exchange(x, axis="replica"):
    return lax.all_to_all(x, axis, split_axis=0, concat_axis=0, tiled=True)


def body(
    hidden,
    base_query,
    key_value_cache,
    adapter_down_weight,
    adapter_up_weight,
    adapter_holder,
    adapter_position,
    request_page_table,
    lengths,
    migration_page_lists,
):
    rows, features = hidden.shape
    peers = lax.axis_size("replica")
    shards = lax.axis_size("tensor")
    heads = features // HEAD
    S = jax.ShapeDtypeStruct
    holder = adapter_holder.reshape(1, rows)
    position = adapter_position.reshape(1, rows)
    table = request_page_table.T
    length = lengths.reshape(1, rows)
    lists = migration_page_lists[0].T
    down = adapter_down_weight.reshape(-1, features)
    up = adapter_up_weight.reshape(-1, features)
    many = down.shape[0]

    ints = lambda n: pltpu.VMEM((n, rows), jnp.int32)
    sent = call(
        send_kernel,
        S((peers, 2, features + HEAD), BF16),
        10**8,
        "hhhhh",
        [pltpu.VMEM((rows, features), BF16), ints(1), ints(1), ints(table.shape[0]), ints(1), pltpu.SemaphoreType.DMA((5,))],
        limit=60,
    )(hidden, holder, position, table, length)
    got = exchange(sent)
    pages, route, start, down = call(
        prepare_kernel,
        (
            S((peers * lists.shape[0] * PAGE, 2 * HEAD), BF16),
            S((2 * peers, peers), BF16),
            S((peers, heads, HEAD), F32),
            S(down.shape, BF16),
        ),
        10**9,
        "svvvvv",
    )(lists, key_value_cache, holder, table, base_query, down)

    partial, pick, limit = call(
        down_kernel,
        (S((shards, RANK, 2 * peers), F32), S((many, 2 * peers), BF16), S((peers, heads, HEAD), F32)),
        10**8,
        "vv",
    )(got, down)
    partials = exchange(partial, "tensor")
    delta = call(up_kernel, S((peers, 2, features), BF16), 10**8, "vvv")(partials, pick, up)
    returned = exchange(delta)
    wide = pltpu.VMEM((rows, heads, HEAD), F32)
    asked = exchange(
        call(query_kernel, S((peers, heads, HEAD), BF16), 10**8, "vvv", (wide,))(returned, route, start)
    )
    local = call(local_kernel, S((rows, features), BF16), 10**9, "ssvvvvv", (wide, wide))(
        table, length, returned, base_query, holder, table, key_value_cache
    )
    answered = exchange(
        call(moved_kernel, S((peers, heads, HEAD), BF16), 10**8, "vvv")(asked, pages, limit)
    )
    return call(final_kernel, S((rows, features), BF16), 10**8, "vvv", (wide,))(answered, local, table)


def solution(mesh):
    in_specs = (
        P("replica", "tensor"),
        P("replica", "tensor"),
        P("replica", None, "tensor"),
        P("replica", None, "tensor"),
        P("replica", None, "tensor"),
        P("replica", None),
        P("replica"),
        P("replica", None),
        P("replica"),
        P("replica", None, None),
    )
    return jax.shard_map(body, mesh=mesh, in_specs=in_specs, out_specs=P("replica", "tensor"), check_vma=False)
```

```python
import jax
import jax.numpy as jnp
from jax import lax
from jax.experimental import pallas as pl
from jax.experimental.pallas import tpu as pltpu
from jax.sharding import PartitionSpec as P

HEAD = 128
RANK = 16
PAGE = 16
POOL = 256
SCALE = 2.0
F32 = jnp.float32
BF16 = jnp.bfloat16
NEG = -1e30
PLANES, DEPTH = 4, 16


def dot(a, b, dims):
    return lax.dot_general(a, b, (dims, ((), ())), preferred_element_type=F32)


def nn(a, b):
    return dot(a, b, ((1,), (0,)))


def nt(a, b):
    return dot(a, b, ((1,), (1,)))


def tn(a, b):
    return dot(a, b, ((0,), (0,)))


def iota(shape, dim):
    return lax.broadcasted_iota(jnp.int32, shape, dim)


def slot_maps(holder_row, peers):
    rows = holder_row.shape[1]
    named = iota((peers, rows), 0) == holder_row
    before = (iota((rows, rows), 0) < iota((rows, rows), 1)).astype(BF16)
    rank = nn(named.astype(BF16), before)
    return [(named & (rank == c)).astype(BF16) for c in range(2)]


def my_plane():
    return lax.div(lax.axis_index("replica"), DEPTH)


def source_at(depth, step):
    return ((my_plane() - step) & (PLANES - 1)) * DEPTH + depth


def moved_from(table, source):
    entry = table[0:1, :]
    return (source == lax.shift_right_arithmetic(entry - POOL, 1)) & (entry >= POOL)


def moved_map(table, peers):
    place = iota((peers, table.shape[1]), 0)
    return moved_from(table, source_at(lax.shift_right_logical(place, 2), place & (PLANES - 1)))


def fetch(pairs, sems):
    copies = [pltpu.make_async_copy(src, dst, sems.at[i]) for i, (src, dst) in enumerate(pairs)]
    for copy in copies:
        copy.start()
    return copies


def send_kernel(
    hidden_hbm, holder_hbm, position_hbm, table_hbm, lengths_hbm, out_ref,
    hidden_ref, holder_ref, position_ref, table_ref, lengths_ref, sems,
):
    peers, _, width = out_ref.shape
    features = width - HEAD
    copies = fetch(
        [
            (holder_hbm, holder_ref),
            (position_hbm, position_ref),
            (table_hbm, table_ref),
            (lengths_hbm, lengths_ref),
            (hidden_hbm, hidden_ref),
        ],
        sems,
    )
    for copy in copies[:4]:
        copy.wait()
    maps = slot_maps(holder_ref[...], peers)
    rows = hidden_ref.shape[0]
    place = (iota((HEAD, rows), 0) == position_ref[...]).astype(BF16)
    lane = iota((peers, HEAD), 1)
    depth = iota((peers, rows), 0) & (DEPTH - 1)
    length = jnp.zeros((peers, HEAD), F32)
    for step in range(PLANES):
        moved = moved_from(table_ref[...], source_at(depth, step))
        total = jnp.sum(jnp.where(moved, lengths_ref[...], 0).astype(F32), axis=1, keepdims=True)
        length = jnp.where(lane >= RANK * (step + 1), total, length)
    for c in range(2):
        out_ref[:, c, features:] = jnp.where(lane < RANK, nt(maps[c], place), length).astype(BF16)
    copies[4].wait()
    hidden = hidden_ref[...]
    for c in range(2):
        out_ref[:, c, :features] = nn(maps[c], hidden).astype(BF16)


def down_kernel(got_ref, down_ref, partial_ref, pick_ref, limit_ref):
    peers, _, width = got_ref.shape
    features = width - HEAD
    many = down_ref.shape[0]
    first, second = got_ref[:, 0, :], got_ref[:, 1, :]
    got = jnp.concatenate([first[:, :features], second[:, :features]], axis=0)
    place = jnp.concatenate([first[:, features:], second[:, features:]], axis=0)
    spread = (lax.shift_right_arithmetic(iota((many, HEAD), 0), 4) == iota((many, HEAD), 1)).astype(BF16)
    pick = nt(spread, place)
    pick_ref[...] = pick.astype(BF16)
    near = got_ref[pl.ds(my_plane() * DEPTH, DEPTH), 0, features:].astype(F32)
    for step in range(PLANES):
        lane = RANK * (step + 1)
        limit_ref[:, step] = jnp.broadcast_to(near[:, lane:lane + 1][:, :, None], limit_ref.shape[:1] + limit_ref.shape[2:])
    projected = nt(down_ref[...], got) * pick
    partial = jnp.sum(projected.reshape(many // RANK, RANK, 2 * peers), axis=0)
    for t in range(partial_ref.shape[0]):
        partial_ref[t] = partial


def up_kernel(got_ref, pick_ref, up_ref, out_ref):
    peers = out_ref.shape[0]
    low = jnp.sum(got_ref[...], axis=0).astype(BF16)
    many = up_ref.shape[0]
    spread = jnp.concatenate([low] * (many // RANK), axis=0) * pick_ref[...]
    delta = (tn(spread, up_ref[...]) * SCALE).astype(BF16)
    for c in range(2):
        out_ref[:, c, :] = delta[c * peers:(c + 1) * peers, :]


def prepare_kernel(
    list_ref, cache_ref, holder_ref, table_ref, base_ref, weight_ref,
    own_ref, one_ref, two_ref, three_ref, route_ref, start_ref, down_ref,
):
    down_ref[...] = weight_ref[...]
    count, owners = list_ref.shape
    for step, page_ref in enumerate((own_ref, one_ref, two_ref, three_ref)):
        first = ((my_plane() + step) & (PLANES - 1)) * DEPTH

        def copy(z, carry, page_ref=page_ref, first=first):
            for k in range(count):
                at = pl.ds(pl.multiple_of((z * count + k) * PAGE, PAGE), PAGE)
                page_ref[at, :] = cache_ref[list_ref[k, first + z]]
            return carry

        lax.fori_loop(0, DEPTH, copy, 0, unroll=8)
    maps = slot_maps(holder_ref[...], owners)
    moved = moved_map(table_ref[...], owners).astype(BF16)
    route_ref[...] = nt(jnp.concatenate(maps, axis=0), moved).astype(BF16)
    start = nn(moved, base_ref[...])
    for h in range(start_ref.shape[1]):
        start_ref[:, h, :] = start[:, h * HEAD:(h + 1) * HEAD]


def query_kernel(got_ref, route_ref, start_ref, one_ref, two_ref, three_ref, out_ref, wide_ref):
    del one_ref, two_ref, three_ref
    got = jnp.concatenate([got_ref[:, 0, :], got_ref[:, 1, :]], axis=0)
    chosen = tn(route_ref[...], got)
    for h in range(wide_ref.shape[1]):
        wide_ref[:, h, :] = chosen[:, h * HEAD:(h + 1) * HEAD]
    out_ref[...] = (start_ref[...] + wide_ref[...]).reshape(out_ref.shape).astype(BF16)


def weighted(scores, live, values):
    scores = jnp.where(live, scores * (HEAD ** -0.5), NEG)
    top = jnp.max(scores, axis=1, keepdims=True)
    weights = jnp.exp(scores - top)
    total = jnp.sum(weights, axis=1, keepdims=True)
    return nn((weights / total).astype(BF16), values)


def local_kernel(
    table_ref, lengths_ref, got_ref, base_ref, holder_ref, row_ref, cache_ref, out_ref, wide_ref, mixed_ref
):
    rows, heads, _ = wide_ref.shape
    pages = table_ref.shape[0]
    span = pages * PAGE
    maps = jnp.concatenate(slot_maps(holder_ref[...], got_ref.shape[0]), axis=0)
    delta = tn(maps, jnp.concatenate([got_ref[:, 0, :], got_ref[:, 1, :]], axis=0))
    query = (base_ref[...].astype(F32) + delta).astype(BF16).astype(F32)
    for h in range(heads):
        wide_ref[:, h, :] = query[:, h * HEAD:(h + 1) * HEAD]
    batch = 4
    shape = (batch * heads, batch * span)
    row_of = lax.div(iota(shape, 0), heads)
    column_of = lax.div(iota(shape, 1), span)
    place = lax.rem(iota(shape, 1), span)
    own = row_of == column_of

    def step(b, carry):
        first = b * batch
        found = []
        limit = jnp.zeros(shape, jnp.int32)
        for i in range(batch):
            limit = jnp.where(row_of == i, lengths_ref[0, first + i], limit)
            for j in range(pages):
                found.append(cache_ref[jnp.minimum(table_ref[j, first + i], POOL - 1)])
        both = jnp.concatenate(found, axis=0)
        q = wide_ref[pl.ds(first, batch)].reshape(batch * heads, HEAD).astype(BF16)
        scores = nt(q, both[:, :HEAD])
        mixed = weighted(scores, own & (place < limit), both[:, HEAD:])
        mixed_ref[pl.ds(first, batch)] = mixed.reshape(batch, heads, HEAD)
        return carry

    lax.fori_loop(0, rows // batch, step, 0, unroll=4)
    stays = jnp.where(row_ref[0:1, :] < POOL, 1.0, 0.0)
    eye = iota((rows, rows), 0) == iota((rows, rows), 1)
    keep = jnp.sum(jnp.where(eye, stays, 0.0), axis=1, keepdims=True)
    for h in range(heads):
        out_ref[:, h * HEAD:(h + 1) * HEAD] = (mixed_ref[:, h, :] * keep).astype(BF16)


def moved_kernel(query_ref, own_ref, one_ref, two_ref, three_ref, limit_ref, out_ref, wide_ref):
    depth, planes, heads, _ = limit_ref.shape
    span = own_ref.shape[0] // depth
    batch = HEAD // span
    wide = batch * heads
    shape = (wide, batch * span)
    own = lax.div(iota(shape, 0), heads) == lax.div(iota(shape, 1), span)
    place = jnp.where(own, lax.rem(iota(shape, 1), span), span).astype(F32)
    query = query_ref[...].astype(F32)
    parts = [(d, z) for d in range(planes) for z in range(0, depth, batch)]
    handed = (own_ref, one_ref, two_ref, three_ref)
    pages = [handed[d][z * span:(z + batch) * span, :] for d, z in parts]
    queries = [
        query[z:z + batch, d * heads:(d + 1) * heads].reshape(wide, HEAD).astype(BF16) for d, z in parts
    ]
    scores = [nt(q, page[:, :HEAD]) for q, page in zip(queries, pages)]
    live = [place < limit_ref[z:z + batch, d].reshape(wide, HEAD) for d, z in parts]
    scores = [jnp.where(m, x * (HEAD ** -0.5), NEG) for m, x in zip(live, scores)]
    tops = [jnp.max(x, axis=1, keepdims=True) for x in scores]
    weights = [jnp.exp(x - top) for x, top in zip(scores, tops)]
    totals = [jnp.sum(x, axis=1, keepdims=True) for x in weights]
    weights = [(x / total).astype(BF16) for x, total in zip(weights, totals)]
    mixed = [nn(x, page[:, HEAD:]) for x, page in zip(weights, pages)]
    for (d, z), x in zip(parts, mixed):
        wide_ref[z:z + batch, d * heads:(d + 1) * heads] = x.reshape(batch, heads, HEAD)
    out_ref[...] = wide_ref[...].astype(BF16)


def final_kernel(got_ref, local_ref, table_ref, out_ref, wide_ref):
    peers, heads, _ = wide_ref.shape
    wide_ref[...] = got_ref[...].astype(F32).reshape(wide_ref.shape)
    moved = moved_map(table_ref[...], peers).astype(BF16)
    for h in range(heads):
        part = tn(moved, wide_ref[:, h, :].astype(BF16))
        at = slice(h * HEAD, (h + 1) * HEAD)
        out_ref[:, at] = (part + local_ref[:, at].astype(F32)).astype(BF16)


def call(kernel, out_shape, cost, spaces, scratch=(), limit=24):
    kinds = {"s": pltpu.SMEM, "v": pltpu.VMEM, "h": pltpu.HBM, "a": pl.ANY}
    return pl.pallas_call(
        kernel,
        out_shape=out_shape,
        in_specs=[pl.BlockSpec(memory_space=kinds[x]) for x in spaces],
        out_specs=jax.tree.map(lambda _: pl.BlockSpec(memory_space=pltpu.VMEM), out_shape),
        scratch_shapes=list(scratch),
        cost_estimate=pl.CostEstimate(flops=cost, bytes_accessed=cost // 100, transcendentals=0),
        compiler_params=pltpu.CompilerParams(vmem_limit_bytes=limit * 1024 * 1024),
    )


def exchange(x, axis="replica", groups=None):
    return lax.all_to_all(x, axis, split_axis=0, concat_axis=0, tiled=True, axis_index_groups=groups)


def along_depth(x):
    return exchange(x, groups=[[p * DEPTH + z for z in range(DEPTH)] for p in range(PLANES)])


def hand_on(x, step):
    pairs = [
        (p * DEPTH + z, (p + step) % PLANES * DEPTH + z) for p in range(PLANES) for z in range(DEPTH)
    ]
    return lax.ppermute(x, "replica", pairs)


def body(
    hidden,
    base_query,
    key_value_cache,
    adapter_down_weight,
    adapter_up_weight,
    adapter_holder,
    adapter_position,
    request_page_table,
    lengths,
    migration_page_lists,
):
    rows, features = hidden.shape
    peers = lax.axis_size("replica")
    shards = lax.axis_size("tensor")
    heads = features // HEAD
    S = jax.ShapeDtypeStruct
    holder = adapter_holder.reshape(1, rows)
    position = adapter_position.reshape(1, rows)
    table = request_page_table.T
    length = lengths.reshape(1, rows)
    lists = migration_page_lists[0].T
    down = adapter_down_weight.reshape(-1, features)
    up = adapter_up_weight.reshape(-1, features)
    many = down.shape[0]

    ints = lambda n: pltpu.VMEM((n, rows), jnp.int32)
    sent = call(
        send_kernel,
        S((peers, 2, features + HEAD), BF16),
        10**8,
        "hhhhh",
        [pltpu.VMEM((rows, features), BF16), ints(1), ints(1), ints(table.shape[0]), ints(1), pltpu.SemaphoreType.DMA((5,))],
        limit=60,
    )(hidden, holder, position, table, length)
    got = exchange(sent)
    handed = S((DEPTH * lists.shape[0] * PAGE, 2 * HEAD), BF16)
    *pages, route, start, down = call(
        prepare_kernel,
        (
            handed,
            handed,
            handed,
            handed,
            S((2 * peers, peers), BF16),
            S((peers, heads, HEAD), F32),
            S(down.shape, BF16),
        ),
        10**9,
        "svvvvv",
    )(lists, key_value_cache, holder, table, base_query, down)
    pages = [pages[0]] + [hand_on(pages[step], step) for step in range(1, PLANES)]

    partial, pick, limit = call(
        down_kernel,
        (S((shards, RANK, 2 * peers), F32), S((many, 2 * peers), BF16), S((DEPTH, PLANES, heads, HEAD), F32)),
        10**8,
        "vv",
    )(got, down)
    partials = exchange(partial, "tensor")
    delta = call(up_kernel, S((peers, 2, features), BF16), 10**8, "vvv")(partials, pick, up)
    returned = exchange(delta)
    wide = pltpu.VMEM((rows, heads, HEAD), F32)
    flat = (DEPTH, PLANES * heads, HEAD)
    asked = along_depth(
        call(query_kernel, S(flat, BF16), 10**8, "vvvaaa", (wide,))(returned, route, start, *pages[1:])
    )
    local = call(local_kernel, S((rows, features), BF16), 10**9, "ssvvvvv", (wide, wide))(
        table, length, returned, base_query, holder, table, key_value_cache
    )
    answered = along_depth(
        call(moved_kernel, S(flat, BF16), 10**8, "vvvvvv", (pltpu.VMEM(flat, F32),))(asked, *pages, limit)
    )
    return call(final_kernel, S((rows, features), BF16), 10**8, "vvv", (wide,))(answered, local, table)


def solution(mesh):
    in_specs = (
        P("replica", "tensor"),
        P("replica", "tensor"),
        P("replica", None, "tensor"),
        P("replica", None, "tensor"),
        P("replica", None, "tensor"),
        P("replica", None),
        P("replica"),
        P("replica", None),
        P("replica"),
        P("replica", None, None),
    )
    return jax.shard_map(body, mesh=mesh, in_specs=in_specs, out_specs=P("replica", "tensor"), check_vma=False)
```

```python
import jax
import jax.numpy as jnp
from jax import lax
from jax.experimental import pallas as pl
from jax.experimental.pallas import tpu as pltpu
from jax.sharding import PartitionSpec as P

HEAD = 128
RANK = 16
PAGE = 16
POOL = 256
SCALE = 2.0
F32 = jnp.float32
BF16 = jnp.bfloat16
NEG = -1e30
PLANES, DEPTH = 4, 16


def dot(a, b, dims):
    return lax.dot_general(a, b, (dims, ((), ())), preferred_element_type=F32)


def nn(a, b):
    return dot(a, b, ((1,), (0,)))


def nt(a, b):
    return dot(a, b, ((1,), (1,)))


def tn(a, b):
    return dot(a, b, ((0,), (0,)))


def iota(shape, dim):
    return lax.broadcasted_iota(jnp.int32, shape, dim)


def slot_maps(holder_row, peers):
    rows = holder_row.shape[1]
    named = iota((peers, rows), 0) == holder_row
    before = (iota((rows, rows), 0) < iota((rows, rows), 1)).astype(BF16)
    rank = nn(named.astype(BF16), before)
    return [(named & (rank == c)).astype(BF16) for c in range(2)]


def my_plane():
    return lax.div(lax.axis_index("replica"), DEPTH)


def source_at(depth, step):
    return ((my_plane() - step) & (PLANES - 1)) * DEPTH + depth


def moved_from(table, source):
    entry = table[0:1, :]
    return (source == lax.shift_right_arithmetic(entry - POOL, 1)) & (entry >= POOL)


def moved_map(table, peers):
    place = iota((peers, table.shape[1]), 0)
    return moved_from(table, source_at(lax.shift_right_logical(place, 2), place & (PLANES - 1)))


def fetch(pairs, sems):
    copies = [pltpu.make_async_copy(src, dst, sems.at[i]) for i, (src, dst) in enumerate(pairs)]
    for copy in copies:
        copy.start()
    return copies


def send_kernel(
    hidden_hbm, holder_hbm, position_hbm, table_hbm, lengths_hbm, out_ref,
    hidden_ref, holder_ref, position_ref, table_ref, lengths_ref, sems,
):
    peers, _, width = out_ref.shape
    features = width - HEAD
    copies = fetch(
        [
            (holder_hbm, holder_ref),
            (position_hbm, position_ref),
            (table_hbm, table_ref),
            (lengths_hbm, lengths_ref),
            (hidden_hbm, hidden_ref),
        ],
        sems,
    )
    for copy in copies[:4]:
        copy.wait()
    maps = slot_maps(holder_ref[...], peers)
    rows = hidden_ref.shape[0]
    place = (iota((HEAD, rows), 0) == position_ref[...]).astype(BF16)
    lane = iota((peers, HEAD), 1)
    depth = iota((peers, rows), 0) & (DEPTH - 1)
    length = jnp.zeros((peers, HEAD), F32)
    for step in range(PLANES):
        moved = moved_from(table_ref[...], source_at(depth, step))
        total = jnp.sum(jnp.where(moved, lengths_ref[...], 0).astype(F32), axis=1, keepdims=True)
        length = jnp.where(lane >= RANK * (step + 1), total, length)
    for c in range(2):
        out_ref[:, c, features:] = jnp.where(lane < RANK, nt(maps[c], place), length).astype(BF16)
    copies[4].wait()
    hidden = hidden_ref[...]
    for c in range(2):
        out_ref[:, c, :features] = nn(maps[c], hidden).astype(BF16)


def down_kernel(got_ref, down_ref, two_ref, partial_ref, pick_ref, limit_ref):
    del two_ref
    peers, _, width = got_ref.shape
    features = width - HEAD
    many = down_ref.shape[0]
    first, second = got_ref[:, 0, :], got_ref[:, 1, :]
    got = jnp.concatenate([first[:, :features], second[:, :features]], axis=0)
    place = jnp.concatenate([first[:, features:], second[:, features:]], axis=0)
    spread = (lax.shift_right_arithmetic(iota((many, HEAD), 0), 4) == iota((many, HEAD), 1)).astype(BF16)
    pick = nt(spread, place)
    pick_ref[...] = pick.astype(BF16)
    near = got_ref[pl.ds(my_plane() * DEPTH, DEPTH), 0, features:].astype(F32)
    for step in range(PLANES):
        lane = RANK * (step + 1)
        limit_ref[:, step] = jnp.broadcast_to(near[:, lane:lane + 1][:, :, None], limit_ref.shape[:1] + limit_ref.shape[2:])
    projected = nt(down_ref[...], got) * pick
    partial = jnp.sum(projected.reshape(many // RANK, RANK, 2 * peers), axis=0)
    for t in range(partial_ref.shape[0]):
        partial_ref[t] = partial


def up_kernel(got_ref, pick_ref, up_ref, out_ref):
    peers = out_ref.shape[0]
    low = jnp.sum(got_ref[...], axis=0).astype(BF16)
    many = up_ref.shape[0]
    spread = jnp.concatenate([low] * (many // RANK), axis=0) * pick_ref[...]
    delta = (tn(spread, up_ref[...]) * SCALE).astype(BF16)
    for c in range(2):
        out_ref[:, c, :] = delta[c * peers:(c + 1) * peers, :]


def prepare_kernel(
    list_ref, cache_ref, holder_ref, table_ref, base_ref, weight_ref,
    own_ref, one_ref, two_ref, three_ref, route_ref, start_ref, down_ref,
):
    down_ref[...] = weight_ref[...]
    count, owners = list_ref.shape
    for step, page_ref in enumerate((own_ref, one_ref, two_ref, three_ref)):
        first = ((my_plane() + step) & (PLANES - 1)) * DEPTH

        def copy(z, carry, page_ref=page_ref, first=first):
            for k in range(count):
                at = pl.ds(pl.multiple_of((z * count + k) * PAGE, PAGE), PAGE)
                page_ref[at, :] = cache_ref[list_ref[k, first + z]]
            return carry

        lax.fori_loop(0, DEPTH, copy, 0, unroll=8)
    maps = slot_maps(holder_ref[...], owners)
    moved = moved_map(table_ref[...], owners).astype(BF16)
    route_ref[...] = nt(jnp.concatenate(maps, axis=0), moved).astype(BF16)
    start = nn(moved, base_ref[...])
    for h in range(start_ref.shape[1]):
        start_ref[:, h, :] = start[:, h * HEAD:(h + 1) * HEAD]


def query_kernel(got_ref, route_ref, start_ref, one_ref, three_ref, out_ref, wide_ref):
    del one_ref, three_ref
    got = jnp.concatenate([got_ref[:, 0, :], got_ref[:, 1, :]], axis=0)
    chosen = tn(route_ref[...], got)
    for h in range(wide_ref.shape[1]):
        wide_ref[:, h, :] = chosen[:, h * HEAD:(h + 1) * HEAD]
    out_ref[...] = (start_ref[...] + wide_ref[...]).reshape(out_ref.shape).astype(BF16)


def weighted(scores, live, values):
    scores = jnp.where(live, scores * (HEAD ** -0.5), NEG)
    top = jnp.max(scores, axis=1, keepdims=True)
    weights = jnp.exp(scores - top)
    total = jnp.sum(weights, axis=1, keepdims=True)
    return nn((weights / total).astype(BF16), values)


def local_kernel(
    table_ref, lengths_ref, got_ref, base_ref, holder_ref, row_ref, cache_ref, out_ref, wide_ref, mixed_ref
):
    rows, heads, _ = wide_ref.shape
    pages = table_ref.shape[0]
    span = pages * PAGE
    maps = jnp.concatenate(slot_maps(holder_ref[...], got_ref.shape[0]), axis=0)
    delta = tn(maps, jnp.concatenate([got_ref[:, 0, :], got_ref[:, 1, :]], axis=0))
    query = (base_ref[...].astype(F32) + delta).astype(BF16).astype(F32)
    for h in range(heads):
        wide_ref[:, h, :] = query[:, h * HEAD:(h + 1) * HEAD]
    batch = 4
    shape = (batch * heads, batch * span)
    row_of = lax.div(iota(shape, 0), heads)
    column_of = lax.div(iota(shape, 1), span)
    place = lax.rem(iota(shape, 1), span)
    own = row_of == column_of

    def step(b, carry):
        first = b * batch
        found = []
        limit = jnp.zeros(shape, jnp.int32)
        for i in range(batch):
            limit = jnp.where(row_of == i, lengths_ref[0, first + i], limit)
            for j in range(pages):
                found.append(cache_ref[jnp.minimum(table_ref[j, first + i], POOL - 1)])
        both = jnp.concatenate(found, axis=0)
        q = wide_ref[pl.ds(first, batch)].reshape(batch * heads, HEAD).astype(BF16)
        scores = nt(q, both[:, :HEAD])
        mixed = weighted(scores, own & (place < limit), both[:, HEAD:])
        mixed_ref[pl.ds(first, batch)] = mixed.reshape(batch, heads, HEAD)
        return carry

    lax.fori_loop(0, rows // batch, step, 0, unroll=4)
    stays = jnp.where(row_ref[0:1, :] < POOL, 1.0, 0.0)
    eye = iota((rows, rows), 0) == iota((rows, rows), 1)
    keep = jnp.sum(jnp.where(eye, stays, 0.0), axis=1, keepdims=True)
    for h in range(heads):
        out_ref[:, h * HEAD:(h + 1) * HEAD] = (mixed_ref[:, h, :] * keep).astype(BF16)


def moved_kernel(query_ref, own_ref, one_ref, two_ref, three_ref, limit_ref, out_ref, wide_ref):
    depth, planes, heads, _ = limit_ref.shape
    span = own_ref.shape[0] // depth
    batch = HEAD // span
    wide = batch * heads
    shape = (wide, batch * span)
    own = lax.div(iota(shape, 0), heads) == lax.div(iota(shape, 1), span)
    place = jnp.where(own, lax.rem(iota(shape, 1), span), span).astype(F32)
    query = query_ref[...].astype(F32)
    parts = [(d, z) for d in range(planes) for z in range(0, depth, batch)]
    handed = (own_ref, one_ref, two_ref, three_ref)
    pages = [handed[d][z * span:(z + batch) * span, :] for d, z in parts]
    queries = [
        query[z:z + batch, d * heads:(d + 1) * heads].reshape(wide, HEAD).astype(BF16) for d, z in parts
    ]
    scores = [nt(q, page[:, :HEAD]) for q, page in zip(queries, pages)]
    live = [place < limit_ref[z:z + batch, d].reshape(wide, HEAD) for d, z in parts]
    scores = [jnp.where(m, x * (HEAD ** -0.5), NEG) for m, x in zip(live, scores)]
    tops = [jnp.max(x, axis=1, keepdims=True) for x in scores]
    weights = [jnp.exp(x - top) for x, top in zip(scores, tops)]
    totals = [jnp.sum(x, axis=1, keepdims=True) for x in weights]
    weights = [(x / total).astype(BF16) for x, total in zip(weights, totals)]
    mixed = [nn(x, page[:, HEAD:]) for x, page in zip(weights, pages)]
    for (d, z), x in zip(parts, mixed):
        wide_ref[z:z + batch, d * heads:(d + 1) * heads] = x.reshape(batch, heads, HEAD)
    out_ref[...] = wide_ref[...].astype(BF16)


def final_kernel(got_ref, local_ref, table_ref, out_ref, wide_ref):
    peers, heads, _ = wide_ref.shape
    wide_ref[...] = got_ref[...].astype(F32).reshape(wide_ref.shape)
    moved = moved_map(table_ref[...], peers).astype(BF16)
    for h in range(heads):
        part = tn(moved, wide_ref[:, h, :].astype(BF16))
        at = slice(h * HEAD, (h + 1) * HEAD)
        out_ref[:, at] = (part + local_ref[:, at].astype(F32)).astype(BF16)


def call(kernel, out_shape, cost, spaces, scratch=(), limit=24):
    kinds = {"s": pltpu.SMEM, "v": pltpu.VMEM, "h": pltpu.HBM, "a": pl.ANY}
    return pl.pallas_call(
        kernel,
        out_shape=out_shape,
        in_specs=[pl.BlockSpec(memory_space=kinds[x]) for x in spaces],
        out_specs=jax.tree.map(lambda _: pl.BlockSpec(memory_space=pltpu.VMEM), out_shape),
        scratch_shapes=list(scratch),
        cost_estimate=pl.CostEstimate(flops=cost, bytes_accessed=cost // 100, transcendentals=0),
        compiler_params=pltpu.CompilerParams(vmem_limit_bytes=limit * 1024 * 1024),
    )


def exchange(x, axis="replica", groups=None):
    return lax.all_to_all(x, axis, split_axis=0, concat_axis=0, tiled=True, axis_index_groups=groups)


def along_depth(x):
    return exchange(x, groups=[[p * DEPTH + z for z in range(DEPTH)] for p in range(PLANES)])


def hand_on(x, step):
    pairs = [
        (p * DEPTH + z, (p + step) % PLANES * DEPTH + z) for p in range(PLANES) for z in range(DEPTH)
    ]
    return lax.ppermute(x, "replica", pairs)


def body(
    hidden,
    base_query,
    key_value_cache,
    adapter_down_weight,
    adapter_up_weight,
    adapter_holder,
    adapter_position,
    request_page_table,
    lengths,
    migration_page_lists,
):
    rows, features = hidden.shape
    peers = lax.axis_size("replica")
    shards = lax.axis_size("tensor")
    heads = features // HEAD
    S = jax.ShapeDtypeStruct
    holder = adapter_holder.reshape(1, rows)
    position = adapter_position.reshape(1, rows)
    table = request_page_table.T
    length = lengths.reshape(1, rows)
    lists = migration_page_lists[0].T
    down = adapter_down_weight.reshape(-1, features)
    up = adapter_up_weight.reshape(-1, features)
    many = down.shape[0]

    ints = lambda n: pltpu.VMEM((n, rows), jnp.int32)
    sent = call(
        send_kernel,
        S((peers, 2, features + HEAD), BF16),
        10**8,
        "hhhhh",
        [pltpu.VMEM((rows, features), BF16), ints(1), ints(1), ints(table.shape[0]), ints(1), pltpu.SemaphoreType.DMA((5,))],
        limit=60,
    )(hidden, holder, position, table, length)
    got = exchange(sent)
    handed = S((DEPTH * lists.shape[0] * PAGE, 2 * HEAD), BF16)
    *pages, route, start, down = call(
        prepare_kernel,
        (
            handed,
            handed,
            handed,
            handed,
            S((2 * peers, peers), BF16),
            S((peers, heads, HEAD), F32),
            S(down.shape, BF16),
        ),
        10**9,
        "svvvvv",
    )(lists, key_value_cache, holder, table, base_query, down)
    pages = [pages[0]] + [hand_on(pages[step], step) for step in range(1, PLANES)]

    partial, pick, limit = call(
        down_kernel,
        (S((shards, RANK, 2 * peers), F32), S((many, 2 * peers), BF16), S((DEPTH, PLANES, heads, HEAD), F32)),
        10**8,
        "vva",
    )(got, down, pages[2])
    partials = exchange(partial, "tensor")
    delta = call(up_kernel, S((peers, 2, features), BF16), 10**8, "vvv")(partials, pick, up)
    returned = exchange(delta)
    wide = pltpu.VMEM((rows, heads, HEAD), F32)
    flat = (DEPTH, PLANES * heads, HEAD)
    asked = along_depth(
        call(query_kernel, S(flat, BF16), 10**8, "vvvaa", (wide,))(returned, route, start, pages[1], pages[3])
    )
    local = call(local_kernel, S((rows, features), BF16), 10**9, "ssvvvvv", (wide, wide))(
        table, length, returned, base_query, holder, table, key_value_cache
    )
    answered = along_depth(
        call(moved_kernel, S(flat, BF16), 10**8, "vvvvvv", (pltpu.VMEM(flat, F32),))(asked, *pages, limit)
    )
    return call(final_kernel, S((rows, features), BF16), 10**8, "vvv", (wide,))(answered, local, table)


def solution(mesh):
    in_specs = (
        P("replica", "tensor"),
        P("replica", "tensor"),
        P("replica", None, "tensor"),
        P("replica", None, "tensor"),
        P("replica", None, "tensor"),
        P("replica", None),
        P("replica"),
        P("replica", None),
        P("replica"),
        P("replica", None, None),
    )
    return jax.shard_map(body, mesh=mesh, in_specs=in_specs, out_specs=P("replica", "tensor"), check_vma=False)
```

```python
import jax
import jax.numpy as jnp
from jax import lax
from jax.experimental import pallas as pl
from jax.experimental.pallas import tpu as pltpu
from jax.sharding import PartitionSpec as P

HEAD = 128
RANK = 16
PAGE = 16
POOL = 256
SCALE = 2.0
F32 = jnp.float32
BF16 = jnp.bfloat16
NEG = -1e30
PLANES, DEPTH = 4, 16


def dot(a, b, dims):
    return lax.dot_general(a, b, (dims, ((), ())), preferred_element_type=F32)


def nn(a, b):
    return dot(a, b, ((1,), (0,)))


def nt(a, b):
    return dot(a, b, ((1,), (1,)))


def tn(a, b):
    return dot(a, b, ((0,), (0,)))


def iota(shape, dim):
    return lax.broadcasted_iota(jnp.int32, shape, dim)


def slot_maps(holder_row, peers):
    rows = holder_row.shape[1]
    named = iota((peers, rows), 0) == holder_row
    before = (iota((rows, rows), 0) < iota((rows, rows), 1)).astype(BF16)
    rank = nn(named.astype(BF16), before)
    return [(named & (rank == c)).astype(BF16) for c in range(2)]


def my_plane():
    return lax.div(lax.axis_index("replica"), DEPTH)


def source_at(depth, step):
    return ((my_plane() - step) & (PLANES - 1)) * DEPTH + depth


def moved_from(table, source):
    entry = table[0:1, :]
    return (source == lax.shift_right_arithmetic(entry - POOL, 1)) & (entry >= POOL)


def moved_map(table, peers):
    place = iota((peers, table.shape[1]), 0)
    return moved_from(table, source_at(lax.shift_right_logical(place, 2), place & (PLANES - 1)))


def fetch(pairs, sems):
    copies = [pltpu.make_async_copy(src, dst, sems.at[i]) for i, (src, dst) in enumerate(pairs)]
    for copy in copies:
        copy.start()
    return copies


def send_kernel(
    hidden_hbm, holder_hbm, position_hbm, table_hbm, lengths_hbm, out_ref,
    hidden_ref, holder_ref, position_ref, table_ref, lengths_ref, sems,
):
    peers, _, width = out_ref.shape
    features = width - HEAD
    copies = fetch(
        [
            (holder_hbm, holder_ref),
            (position_hbm, position_ref),
            (table_hbm, table_ref),
            (lengths_hbm, lengths_ref),
            (hidden_hbm, hidden_ref),
        ],
        sems,
    )
    for copy in copies[:4]:
        copy.wait()
    maps = slot_maps(holder_ref[...], peers)
    rows = hidden_ref.shape[0]
    place = (iota((HEAD, rows), 0) == position_ref[...]).astype(BF16)
    lane = iota((peers, HEAD), 1)
    depth = iota((peers, rows), 0) & (DEPTH - 1)
    length = jnp.zeros((peers, HEAD), F32)
    for step in range(PLANES):
        moved = moved_from(table_ref[...], source_at(depth, step))
        total = jnp.sum(jnp.where(moved, lengths_ref[...], 0).astype(F32), axis=1, keepdims=True)
        length = jnp.where(lane >= RANK * (step + 1), total, length)
    for c in range(2):
        out_ref[:, c, features:] = jnp.where(lane < RANK, nt(maps[c], place), length).astype(BF16)
    copies[4].wait()
    hidden = hidden_ref[...]
    for c in range(2):
        out_ref[:, c, :features] = nn(maps[c], hidden).astype(BF16)


def down_kernel(got_ref, down_ref, one_ref, partial_ref, pick_ref, limit_ref):
    del one_ref
    peers, _, width = got_ref.shape
    features = width - HEAD
    many = down_ref.shape[0]
    first, second = got_ref[:, 0, :], got_ref[:, 1, :]
    got = jnp.concatenate([first[:, :features], second[:, :features]], axis=0)
    place = jnp.concatenate([first[:, features:], second[:, features:]], axis=0)
    spread = (lax.shift_right_arithmetic(iota((many, HEAD), 0), 4) == iota((many, HEAD), 1)).astype(BF16)
    pick = nt(spread, place)
    pick_ref[...] = pick.astype(BF16)
    near = got_ref[pl.ds(my_plane() * DEPTH, DEPTH), 0, features:].astype(F32)
    for step in range(PLANES):
        lane = RANK * (step + 1)
        limit_ref[:, step] = jnp.broadcast_to(near[:, lane:lane + 1][:, :, None], limit_ref.shape[:1] + limit_ref.shape[2:])
    projected = nt(down_ref[...], got) * pick
    partial = jnp.sum(projected.reshape(many // RANK, RANK, 2 * peers), axis=0)
    for t in range(partial_ref.shape[0]):
        partial_ref[t] = partial


def up_kernel(got_ref, pick_ref, up_ref, out_ref):
    peers = out_ref.shape[0]
    low = jnp.sum(got_ref[...], axis=0).astype(BF16)
    many = up_ref.shape[0]
    spread = jnp.concatenate([low] * (many // RANK), axis=0) * pick_ref[...]
    delta = (tn(spread, up_ref[...]) * SCALE).astype(BF16)
    for c in range(2):
        out_ref[:, c, :] = delta[c * peers:(c + 1) * peers, :]


def gather_kernel(list_ref, cache_ref, own_ref, one_ref, two_ref, three_ref):
    count = list_ref.shape[0]
    for step, page_ref in enumerate((own_ref, one_ref, two_ref, three_ref)):
        first = ((my_plane() + step) & (PLANES - 1)) * DEPTH

        def copy(z, carry, page_ref=page_ref, first=first):
            for k in range(count):
                at = pl.ds(pl.multiple_of((z * count + k) * PAGE, PAGE), PAGE)
                page_ref[at, :] = cache_ref[list_ref[k, first + z]]
            return carry

        lax.fori_loop(0, DEPTH, copy, 0, unroll=8)


def prepare_kernel(holder_ref, table_ref, base_ref, weight_ref, route_ref, start_ref, down_ref):
    down_ref[...] = weight_ref[...]
    owners = route_ref.shape[1]
    maps = slot_maps(holder_ref[...], owners)
    moved = moved_map(table_ref[...], owners).astype(BF16)
    route_ref[...] = nt(jnp.concatenate(maps, axis=0), moved).astype(BF16)
    start = nn(moved, base_ref[...])
    for h in range(start_ref.shape[1]):
        start_ref[:, h, :] = start[:, h * HEAD:(h + 1) * HEAD]


def query_kernel(got_ref, route_ref, start_ref, two_ref, three_ref, out_ref, wide_ref):
    del two_ref, three_ref
    got = jnp.concatenate([got_ref[:, 0, :], got_ref[:, 1, :]], axis=0)
    chosen = tn(route_ref[...], got)
    for h in range(wide_ref.shape[1]):
        wide_ref[:, h, :] = chosen[:, h * HEAD:(h + 1) * HEAD]
    out_ref[...] = (start_ref[...] + wide_ref[...]).reshape(out_ref.shape).astype(BF16)


def weighted(scores, live, values):
    scores = jnp.where(live, scores * (HEAD ** -0.5), NEG)
    top = jnp.max(scores, axis=1, keepdims=True)
    weights = jnp.exp(scores - top)
    total = jnp.sum(weights, axis=1, keepdims=True)
    return nn((weights / total).astype(BF16), values)


def local_kernel(
    table_ref, lengths_ref, got_ref, base_ref, holder_ref, row_ref, cache_ref, out_ref, wide_ref, mixed_ref
):
    rows, heads, _ = wide_ref.shape
    pages = table_ref.shape[0]
    span = pages * PAGE
    maps = jnp.concatenate(slot_maps(holder_ref[...], got_ref.shape[0]), axis=0)
    delta = tn(maps, jnp.concatenate([got_ref[:, 0, :], got_ref[:, 1, :]], axis=0))
    query = (base_ref[...].astype(F32) + delta).astype(BF16).astype(F32)
    for h in range(heads):
        wide_ref[:, h, :] = query[:, h * HEAD:(h + 1) * HEAD]
    batch = 4
    shape = (batch * heads, batch * span)
    row_of = lax.div(iota(shape, 0), heads)
    column_of = lax.div(iota(shape, 1), span)
    place = lax.rem(iota(shape, 1), span)
    own = row_of == column_of

    def step(b, carry):
        first = b * batch
        found = []
        limit = jnp.zeros(shape, jnp.int32)
        for i in range(batch):
            limit = jnp.where(row_of == i, lengths_ref[0, first + i], limit)
            for j in range(pages):
                found.append(cache_ref[jnp.minimum(table_ref[j, first + i], POOL - 1)])
        both = jnp.concatenate(found, axis=0)
        q = wide_ref[pl.ds(first, batch)].reshape(batch * heads, HEAD).astype(BF16)
        scores = nt(q, both[:, :HEAD])
        mixed = weighted(scores, own & (place < limit), both[:, HEAD:])
        mixed_ref[pl.ds(first, batch)] = mixed.reshape(batch, heads, HEAD)
        return carry

    lax.fori_loop(0, rows // batch, step, 0, unroll=4)
    stays = jnp.where(row_ref[0:1, :] < POOL, 1.0, 0.0)
    eye = iota((rows, rows), 0) == iota((rows, rows), 1)
    keep = jnp.sum(jnp.where(eye, stays, 0.0), axis=1, keepdims=True)
    for h in range(heads):
        out_ref[:, h * HEAD:(h + 1) * HEAD] = (mixed_ref[:, h, :] * keep).astype(BF16)


def moved_kernel(query_ref, own_ref, one_ref, two_ref, three_ref, limit_ref, out_ref, wide_ref):
    depth, planes, heads, _ = limit_ref.shape
    span = own_ref.shape[0] // depth
    batch = HEAD // span
    wide = batch * heads
    shape = (wide, batch * span)
    own = lax.div(iota(shape, 0), heads) == lax.div(iota(shape, 1), span)
    place = jnp.where(own, lax.rem(iota(shape, 1), span), span).astype(F32)
    query = query_ref[...].astype(F32)
    parts = [(d, z) for d in range(planes) for z in range(0, depth, batch)]
    handed = (own_ref, one_ref, two_ref, three_ref)
    pages = [handed[d][z * span:(z + batch) * span, :] for d, z in parts]
    queries = [
        query[z:z + batch, d * heads:(d + 1) * heads].reshape(wide, HEAD).astype(BF16) for d, z in parts
    ]
    scores = [nt(q, page[:, :HEAD]) for q, page in zip(queries, pages)]
    live = [place < limit_ref[z:z + batch, d].reshape(wide, HEAD) for d, z in parts]
    scores = [jnp.where(m, x * (HEAD ** -0.5), NEG) for m, x in zip(live, scores)]
    tops = [jnp.max(x, axis=1, keepdims=True) for x in scores]
    weights = [jnp.exp(x - top) for x, top in zip(scores, tops)]
    totals = [jnp.sum(x, axis=1, keepdims=True) for x in weights]
    weights = [(x / total).astype(BF16) for x, total in zip(weights, totals)]
    mixed = [nn(x, page[:, HEAD:]) for x, page in zip(weights, pages)]
    for (d, z), x in zip(parts, mixed):
        wide_ref[z:z + batch, d * heads:(d + 1) * heads] = x.reshape(batch, heads, HEAD)
    out_ref[...] = wide_ref[...].astype(BF16)


def final_kernel(got_ref, local_ref, table_ref, out_ref, wide_ref):
    peers, heads, _ = wide_ref.shape
    wide_ref[...] = got_ref[...].astype(F32).reshape(wide_ref.shape)
    moved = moved_map(table_ref[...], peers).astype(BF16)
    for h in range(heads):
        part = tn(moved, wide_ref[:, h, :].astype(BF16))
        at = slice(h * HEAD, (h + 1) * HEAD)
        out_ref[:, at] = (part + local_ref[:, at].astype(F32)).astype(BF16)


def call(kernel, out_shape, cost, spaces, scratch=(), limit=24):
    kinds = {"s": pltpu.SMEM, "v": pltpu.VMEM, "h": pltpu.HBM, "a": pl.ANY}
    return pl.pallas_call(
        kernel,
        out_shape=out_shape,
        in_specs=[pl.BlockSpec(memory_space=kinds[x]) for x in spaces],
        out_specs=jax.tree.map(lambda _: pl.BlockSpec(memory_space=pltpu.VMEM), out_shape),
        scratch_shapes=list(scratch),
        cost_estimate=pl.CostEstimate(flops=cost, bytes_accessed=cost // 100, transcendentals=0),
        compiler_params=pltpu.CompilerParams(vmem_limit_bytes=limit * 1024 * 1024),
    )


def exchange(x, axis="replica", groups=None):
    return lax.all_to_all(x, axis, split_axis=0, concat_axis=0, tiled=True, axis_index_groups=groups)


def along_depth(x):
    return exchange(x, groups=[[p * DEPTH + z for z in range(DEPTH)] for p in range(PLANES)])


def hand_on(x, step):
    pairs = [
        (p * DEPTH + z, (p + step) % PLANES * DEPTH + z) for p in range(PLANES) for z in range(DEPTH)
    ]
    return lax.ppermute(x, "replica", pairs)


def body(
    hidden,
    base_query,
    key_value_cache,
    adapter_down_weight,
    adapter_up_weight,
    adapter_holder,
    adapter_position,
    request_page_table,
    lengths,
    migration_page_lists,
):
    rows, features = hidden.shape
    peers = lax.axis_size("replica")
    shards = lax.axis_size("tensor")
    heads = features // HEAD
    S = jax.ShapeDtypeStruct
    holder = adapter_holder.reshape(1, rows)
    position = adapter_position.reshape(1, rows)
    table = request_page_table.T
    length = lengths.reshape(1, rows)
    lists = migration_page_lists[0].T
    down = adapter_down_weight.reshape(-1, features)
    up = adapter_up_weight.reshape(-1, features)
    many = down.shape[0]

    ints = lambda n: pltpu.VMEM((n, rows), jnp.int32)
    sent = call(
        send_kernel,
        S((peers, 2, features + HEAD), BF16),
        10**8,
        "hhhhh",
        [pltpu.VMEM((rows, features), BF16), ints(1), ints(1), ints(table.shape[0]), ints(1), pltpu.SemaphoreType.DMA((5,))],
        limit=60,
    )(hidden, holder, position, table, length)
    got = exchange(sent)
    handed = S((DEPTH * lists.shape[0] * PAGE, 2 * HEAD), BF16)
    pages = call(gather_kernel, (handed,) * PLANES, 10**9, "sv")(lists, key_value_cache)
    route, start, down = call(
        prepare_kernel,
        (S((2 * peers, peers), BF16), S((peers, heads, HEAD), F32), S(down.shape, BF16)),
        10**8,
        "vvvv",
    )(holder, table, base_query, down)
    pages = [pages[0]] + [hand_on(pages[step], step) for step in range(1, PLANES)]

    partial, pick, limit = call(
        down_kernel,
        (S((shards, RANK, 2 * peers), F32), S((many, 2 * peers), BF16), S((DEPTH, PLANES, heads, HEAD), F32)),
        10**8,
        "vva",
    )(got, down, pages[1])
    partials = exchange(partial, "tensor")
    delta = call(up_kernel, S((peers, 2, features), BF16), 10**8, "vvv")(partials, pick, up)
    returned = exchange(delta)
    wide = pltpu.VMEM((rows, heads, HEAD), F32)
    flat = (DEPTH, PLANES * heads, HEAD)
    asked = along_depth(
        call(query_kernel, S(flat, BF16), 10**8, "vvvaa", (wide,))(returned, route, start, pages[2], pages[3])
    )
    local = call(local_kernel, S((rows, features), BF16), 10**9, "ssvvvvv", (wide, wide))(
        table, length, returned, base_query, holder, table, key_value_cache
    )
    answered = along_depth(
        call(moved_kernel, S(flat, BF16), 10**8, "vvvvvv", (pltpu.VMEM(flat, F32),))(asked, *pages, limit)
    )
    return call(final_kernel, S((rows, features), BF16), 10**8, "vvv", (wide,))(answered, local, table)


def solution(mesh):
    in_specs = (
        P("replica", "tensor"),
        P("replica", "tensor"),
        P("replica", None, "tensor"),
        P("replica", None, "tensor"),
        P("replica", None, "tensor"),
        P("replica", None),
        P("replica"),
        P("replica", None),
        P("replica"),
        P("replica", None, None),
    )
    return jax.shard_map(body, mesh=mesh, in_specs=in_specs, out_specs=P("replica", "tensor"), check_vma=False)
```

```python
import jax
import jax.numpy as jnp
from jax import lax
from jax.experimental import pallas as pl
from jax.experimental.pallas import tpu as pltpu
from jax.sharding import PartitionSpec as P

HEAD = 128
RANK = 16
PAGE = 16
POOL = 256
SCALE = 2.0
F32 = jnp.float32
BF16 = jnp.bfloat16
NEG = -1e30
PLANES, DEPTH = 4, 16


def dot(a, b, dims):
    return lax.dot_general(a, b, (dims, ((), ())), preferred_element_type=F32)


def nn(a, b):
    return dot(a, b, ((1,), (0,)))


def nt(a, b):
    return dot(a, b, ((1,), (1,)))


def tn(a, b):
    return dot(a, b, ((0,), (0,)))


def iota(shape, dim):
    return lax.broadcasted_iota(jnp.int32, shape, dim)


def slot_maps(holder_row, peers):
    rows = holder_row.shape[1]
    named = iota((peers, rows), 0) == holder_row
    before = (iota((rows, rows), 0) < iota((rows, rows), 1)).astype(BF16)
    rank = nn(named.astype(BF16), before)
    return [(named & (rank == c)).astype(BF16) for c in range(2)]


def my_plane():
    return lax.div(lax.axis_index("replica"), DEPTH)


def source_at(depth, step):
    return ((my_plane() - step) & (PLANES - 1)) * DEPTH + depth


def moved_from(table, source):
    entry = table[0:1, :]
    return (source == lax.shift_right_arithmetic(entry - POOL, 1)) & (entry >= POOL)


def moved_map(table, peers):
    place = iota((peers, table.shape[1]), 0)
    return moved_from(table, source_at(lax.shift_right_logical(place, 2), place & (PLANES - 1)))


def fetch(pairs, sems):
    copies = [pltpu.make_async_copy(src, dst, sems.at[i]) for i, (src, dst) in enumerate(pairs)]
    for copy in copies:
        copy.start()
    return copies


def send_kernel(
    hidden_hbm, holder_hbm, position_hbm, table_hbm, lengths_hbm, out_ref,
    hidden_ref, holder_ref, position_ref, table_ref, lengths_ref, sems,
):
    peers, _, width = out_ref.shape
    features = width - HEAD
    copies = fetch(
        [
            (holder_hbm, holder_ref),
            (position_hbm, position_ref),
            (table_hbm, table_ref),
            (lengths_hbm, lengths_ref),
            (hidden_hbm, hidden_ref),
        ],
        sems,
    )
    for copy in copies[:4]:
        copy.wait()
    maps = slot_maps(holder_ref[...], peers)
    rows = hidden_ref.shape[0]
    place = (iota((HEAD, rows), 0) == position_ref[...]).astype(BF16)
    lane = iota((peers, HEAD), 1)
    depth = iota((peers, rows), 0) & (DEPTH - 1)
    length = jnp.zeros((peers, HEAD), F32)
    for step in range(PLANES):
        moved = moved_from(table_ref[...], source_at(depth, step))
        total = jnp.sum(jnp.where(moved, lengths_ref[...], 0).astype(F32), axis=1, keepdims=True)
        length = jnp.where(lane >= RANK * (step + 1), total, length)
    for c in range(2):
        out_ref[:, c, features:] = jnp.where(lane < RANK, nt(maps[c], place), length).astype(BF16)
    copies[4].wait()
    hidden = hidden_ref[...]
    for c in range(2):
        out_ref[:, c, :features] = nn(maps[c], hidden).astype(BF16)


def down_kernel(got_ref, down_ref, one_ref, partial_ref, pick_ref, limit_ref):
    del one_ref
    peers, _, width = got_ref.shape
    features = width - HEAD
    many = down_ref.shape[0]
    first, second = got_ref[:, 0, :], got_ref[:, 1, :]
    got = jnp.concatenate([first[:, :features], second[:, :features]], axis=0)
    place = jnp.concatenate([first[:, features:], second[:, features:]], axis=0)
    spread = (lax.shift_right_arithmetic(iota((many, HEAD), 0), 4) == iota((many, HEAD), 1)).astype(BF16)
    pick = nt(spread, place)
    pick_ref[...] = pick.astype(BF16)
    near = got_ref[pl.ds(my_plane() * DEPTH, DEPTH), 0, features:].astype(F32)
    for step in range(PLANES):
        lane = RANK * (step + 1)
        limit_ref[:, step] = jnp.broadcast_to(near[:, lane:lane + 1][:, :, None], limit_ref.shape[:1] + limit_ref.shape[2:])
    projected = nt(down_ref[...], got) * pick
    partial = jnp.sum(projected.reshape(many // RANK, RANK, 2 * peers), axis=0)
    for t in range(partial_ref.shape[0]):
        partial_ref[t] = partial


def up_kernel(got_ref, pick_ref, up_ref, out_ref):
    peers = out_ref.shape[0]
    low = jnp.sum(got_ref[...], axis=0).astype(BF16)
    many = up_ref.shape[0]
    spread = jnp.concatenate([low] * (many // RANK), axis=0) * pick_ref[...]
    delta = (tn(spread, up_ref[...]) * SCALE).astype(BF16)
    for c in range(2):
        out_ref[:, c, :] = delta[c * peers:(c + 1) * peers, :]


def gather_kernel(list_ref, cache_ref, own_ref, one_ref, fore_ref, back_ref, three_ref):
    count = list_ref.shape[0]
    half = DEPTH // 2
    for step, low, page_ref in ((0, 0, own_ref), (1, 0, one_ref), (2, 0, fore_ref), (2, half, back_ref), (3, 0, three_ref)):
        first = ((my_plane() + step) & (PLANES - 1)) * DEPTH + low

        def copy(z, carry, page_ref=page_ref, first=first):
            for k in range(count):
                at = pl.ds(pl.multiple_of((z * count + k) * PAGE, PAGE), PAGE)
                page_ref[at, :] = cache_ref[list_ref[k, first + z]]
            return carry

        lax.fori_loop(0, page_ref.shape[0] // (count * PAGE), copy, 0, unroll=8)


def prepare_kernel(holder_ref, table_ref, base_ref, weight_ref, route_ref, start_ref, down_ref):
    down_ref[...] = weight_ref[...]
    owners = route_ref.shape[1]
    maps = slot_maps(holder_ref[...], owners)
    moved = moved_map(table_ref[...], owners).astype(BF16)
    route_ref[...] = nt(jnp.concatenate(maps, axis=0), moved).astype(BF16)
    start = nn(moved, base_ref[...])
    for h in range(start_ref.shape[1]):
        start_ref[:, h, :] = start[:, h * HEAD:(h + 1) * HEAD]


def query_kernel(got_ref, route_ref, start_ref, fore_ref, back_ref, three_ref, out_ref, wide_ref):
    del fore_ref, back_ref, three_ref
    got = jnp.concatenate([got_ref[:, 0, :], got_ref[:, 1, :]], axis=0)
    chosen = tn(route_ref[...], got)
    for h in range(wide_ref.shape[1]):
        wide_ref[:, h, :] = chosen[:, h * HEAD:(h + 1) * HEAD]
    out_ref[...] = (start_ref[...] + wide_ref[...]).reshape(out_ref.shape).astype(BF16)


def weighted(scores, live, values):
    scores = jnp.where(live, scores * (HEAD ** -0.5), NEG)
    top = jnp.max(scores, axis=1, keepdims=True)
    weights = jnp.exp(scores - top)
    total = jnp.sum(weights, axis=1, keepdims=True)
    return nn((weights / total).astype(BF16), values)


def local_kernel(
    table_ref, lengths_ref, got_ref, base_ref, holder_ref, row_ref, cache_ref, out_ref, wide_ref, mixed_ref
):
    rows, heads, _ = wide_ref.shape
    pages = table_ref.shape[0]
    span = pages * PAGE
    maps = jnp.concatenate(slot_maps(holder_ref[...], got_ref.shape[0]), axis=0)
    delta = tn(maps, jnp.concatenate([got_ref[:, 0, :], got_ref[:, 1, :]], axis=0))
    query = (base_ref[...].astype(F32) + delta).astype(BF16).astype(F32)
    for h in range(heads):
        wide_ref[:, h, :] = query[:, h * HEAD:(h + 1) * HEAD]
    batch = 4
    shape = (batch * heads, batch * span)
    row_of = lax.div(iota(shape, 0), heads)
    column_of = lax.div(iota(shape, 1), span)
    place = lax.rem(iota(shape, 1), span)
    own = row_of == column_of

    def step(b, carry):
        first = b * batch
        found = []
        limit = jnp.zeros(shape, jnp.int32)
        for i in range(batch):
            limit = jnp.where(row_of == i, lengths_ref[0, first + i], limit)
            for j in range(pages):
                found.append(cache_ref[jnp.minimum(table_ref[j, first + i], POOL - 1)])
        both = jnp.concatenate(found, axis=0)
        q = wide_ref[pl.ds(first, batch)].reshape(batch * heads, HEAD).astype(BF16)
        scores = nt(q, both[:, :HEAD])
        mixed = weighted(scores, own & (place < limit), both[:, HEAD:])
        mixed_ref[pl.ds(first, batch)] = mixed.reshape(batch, heads, HEAD)
        return carry

    lax.fori_loop(0, rows // batch, step, 0, unroll=4)
    stays = jnp.where(row_ref[0:1, :] < POOL, 1.0, 0.0)
    eye = iota((rows, rows), 0) == iota((rows, rows), 1)
    keep = jnp.sum(jnp.where(eye, stays, 0.0), axis=1, keepdims=True)
    for h in range(heads):
        out_ref[:, h * HEAD:(h + 1) * HEAD] = (mixed_ref[:, h, :] * keep).astype(BF16)


def moved_kernel(query_ref, own_ref, one_ref, fore_ref, back_ref, three_ref, limit_ref, out_ref, wide_ref):
    depth, planes, heads, _ = limit_ref.shape
    span = own_ref.shape[0] // depth
    batch = HEAD // span
    wide = batch * heads
    shape = (wide, batch * span)
    own = lax.div(iota(shape, 0), heads) == lax.div(iota(shape, 1), span)
    place = jnp.where(own, lax.rem(iota(shape, 1), span), span).astype(F32)
    query = query_ref[...].astype(F32)
    parts = [(d, z) for d in range(planes) for z in range(0, depth, batch)]
    handed = ((own_ref,), (one_ref,), (fore_ref, back_ref), (three_ref,))
    pages = []
    for d, z in parts:
        each = depth // len(handed[d])
        first = z % each * span
        pages.append(handed[d][z // each][first:first + batch * span, :])
    queries = [
        query[z:z + batch, d * heads:(d + 1) * heads].reshape(wide, HEAD).astype(BF16) for d, z in parts
    ]
    scores = [nt(q, page[:, :HEAD]) for q, page in zip(queries, pages)]
    live = [place < limit_ref[z:z + batch, d].reshape(wide, HEAD) for d, z in parts]
    scores = [jnp.where(m, x * (HEAD ** -0.5), NEG) for m, x in zip(live, scores)]
    tops = [jnp.max(x, axis=1, keepdims=True) for x in scores]
    weights = [jnp.exp(x - top) for x, top in zip(scores, tops)]
    totals = [jnp.sum(x, axis=1, keepdims=True) for x in weights]
    weights = [(x / total).astype(BF16) for x, total in zip(weights, totals)]
    mixed = [nn(x, page[:, HEAD:]) for x, page in zip(weights, pages)]
    for (d, z), x in zip(parts, mixed):
        wide_ref[z:z + batch, d * heads:(d + 1) * heads] = x.reshape(batch, heads, HEAD)
    out_ref[...] = wide_ref[...].astype(BF16)


def final_kernel(got_ref, local_ref, table_ref, out_ref, wide_ref):
    peers, heads, _ = wide_ref.shape
    wide_ref[...] = got_ref[...].astype(F32).reshape(wide_ref.shape)
    moved = moved_map(table_ref[...], peers).astype(BF16)
    for h in range(heads):
        part = tn(moved, wide_ref[:, h, :].astype(BF16))
        at = slice(h * HEAD, (h + 1) * HEAD)
        out_ref[:, at] = (part + local_ref[:, at].astype(F32)).astype(BF16)


def call(kernel, out_shape, cost, spaces, scratch=(), limit=24):
    kinds = {"s": pltpu.SMEM, "v": pltpu.VMEM, "h": pltpu.HBM, "a": pl.ANY}
    return pl.pallas_call(
        kernel,
        out_shape=out_shape,
        in_specs=[pl.BlockSpec(memory_space=kinds[x]) for x in spaces],
        out_specs=jax.tree.map(lambda _: pl.BlockSpec(memory_space=pltpu.VMEM), out_shape),
        scratch_shapes=list(scratch),
        cost_estimate=pl.CostEstimate(flops=cost, bytes_accessed=cost // 100, transcendentals=0),
        compiler_params=pltpu.CompilerParams(vmem_limit_bytes=limit * 1024 * 1024),
    )


def exchange(x, axis="replica", groups=None):
    return lax.all_to_all(x, axis, split_axis=0, concat_axis=0, tiled=True, axis_index_groups=groups)


def along_depth(x):
    return exchange(x, groups=[[p * DEPTH + z for z in range(DEPTH)] for p in range(PLANES)])


def hand_on(x, step):
    pairs = [
        (p * DEPTH + z, (p + step) % PLANES * DEPTH + z) for p in range(PLANES) for z in range(DEPTH)
    ]
    return lax.ppermute(x, "replica", pairs)


def body(
    hidden,
    base_query,
    key_value_cache,
    adapter_down_weight,
    adapter_up_weight,
    adapter_holder,
    adapter_position,
    request_page_table,
    lengths,
    migration_page_lists,
):
    rows, features = hidden.shape
    peers = lax.axis_size("replica")
    shards = lax.axis_size("tensor")
    heads = features // HEAD
    S = jax.ShapeDtypeStruct
    holder = adapter_holder.reshape(1, rows)
    position = adapter_position.reshape(1, rows)
    table = request_page_table.T
    length = lengths.reshape(1, rows)
    lists = migration_page_lists[0].T
    down = adapter_down_weight.reshape(-1, features)
    up = adapter_up_weight.reshape(-1, features)
    many = down.shape[0]

    ints = lambda n: pltpu.VMEM((n, rows), jnp.int32)
    sent = call(
        send_kernel,
        S((peers, 2, features + HEAD), BF16),
        10**8,
        "hhhhh",
        [pltpu.VMEM((rows, features), BF16), ints(1), ints(1), ints(table.shape[0]), ints(1), pltpu.SemaphoreType.DMA((5,))],
        limit=60,
    )(hidden, holder, position, table, length)
    got = exchange(sent)
    handed = S((DEPTH * lists.shape[0] * PAGE, 2 * HEAD), BF16)
    part = S((handed.shape[0] // 2, 2 * HEAD), BF16)
    own, one, fore, back, three = call(gather_kernel, (handed, handed, part, part, handed), 10**9, "sv")(
        lists, key_value_cache
    )
    one, three = hand_on(one, 1), hand_on(three, -1)
    fore, back = hand_on(fore, 1), hand_on(back, -1)
    route, start, down = call(
        prepare_kernel,
        (S((2 * peers, peers), BF16), S((peers, heads, HEAD), F32), S(down.shape, BF16)),
        10**8,
        "vvvv",
    )(holder, table, base_query, down)

    partial, pick, limit = call(
        down_kernel,
        (S((shards, RANK, 2 * peers), F32), S((many, 2 * peers), BF16), S((DEPTH, PLANES, heads, HEAD), F32)),
        10**8,
        "vva",
    )(got, down, one)
    partials = exchange(partial, "tensor")
    delta = call(up_kernel, S((peers, 2, features), BF16), 10**8, "vvv")(partials, pick, up)
    returned = exchange(delta)
    wide = pltpu.VMEM((rows, heads, HEAD), F32)
    flat = (DEPTH, PLANES * heads, HEAD)
    asked = along_depth(
        call(query_kernel, S(flat, BF16), 10**8, "vvvaaa", (wide,))(returned, route, start, fore, back, three)
    )
    local = call(local_kernel, S((rows, features), BF16), 10**9, "ssvvvvv", (wide, wide))(
        table, length, returned, base_query, holder, table, key_value_cache
    )
    answered = along_depth(
        call(moved_kernel, S(flat, BF16), 10**8, "vvvvvvv", (pltpu.VMEM(flat, F32),))(
            asked, own, one, hand_on(fore, 1), hand_on(back, -1), three, limit
        )
    )
    return call(final_kernel, S((rows, features), BF16), 10**8, "vvv", (wide,))(answered, local, table)


def solution(mesh):
    in_specs = (
        P("replica", "tensor"),
        P("replica", "tensor"),
        P("replica", None, "tensor"),
        P("replica", None, "tensor"),
        P("replica", None, "tensor"),
        P("replica", None),
        P("replica"),
        P("replica", None),
        P("replica"),
        P("replica", None, None),
    )
    return jax.shard_map(body, mesh=mesh, in_specs=in_specs, out_specs=P("replica", "tensor"), check_vma=False)
```

```python
import jax
import jax.numpy as jnp
from jax import lax
from jax.experimental import pallas as pl
from jax.experimental.pallas import tpu as pltpu
from jax.sharding import PartitionSpec as P

HEAD = 128
RANK = 16
PAGE = 16
POOL = 256
SCALE = 2.0
F32 = jnp.float32
BF16 = jnp.bfloat16
NEG = -1e30
PLANES, DEPTH = 4, 16


def dot(a, b, dims):
    return lax.dot_general(a, b, (dims, ((), ())), preferred_element_type=F32)


def nn(a, b):
    return dot(a, b, ((1,), (0,)))


def nt(a, b):
    return dot(a, b, ((1,), (1,)))


def tn(a, b):
    return dot(a, b, ((0,), (0,)))


def iota(shape, dim):
    return lax.broadcasted_iota(jnp.int32, shape, dim)


def slot_maps(holder_row, peers):
    rows = holder_row.shape[1]
    named = iota((peers, rows), 0) == holder_row
    before = (iota((rows, rows), 0) < iota((rows, rows), 1)).astype(BF16)
    rank = nn(named.astype(BF16), before)
    return [(named & (rank == c)).astype(BF16) for c in range(2)]


def my_plane():
    return lax.div(lax.axis_index("replica"), DEPTH)


def source_at(depth, step):
    return ((my_plane() - step) & (PLANES - 1)) * DEPTH + depth


def moved_from(table, source):
    entry = table[0:1, :]
    return (source == lax.shift_right_arithmetic(entry - POOL, 1)) & (entry >= POOL)


def moved_map(table, peers):
    place = iota((peers, table.shape[1]), 0)
    return moved_from(table, source_at(lax.shift_right_logical(place, 2), place & (PLANES - 1)))


def fetch(pairs, sems):
    copies = [pltpu.make_async_copy(src, dst, sems.at[i]) for i, (src, dst) in enumerate(pairs)]
    for copy in copies:
        copy.start()
    return copies


def send_kernel(
    hidden_hbm, holder_hbm, position_hbm, table_hbm, lengths_hbm, out_ref,
    hidden_ref, holder_ref, position_ref, table_ref, lengths_ref, sems,
):
    peers, _, width = out_ref.shape
    features = width - HEAD
    copies = fetch(
        [
            (holder_hbm, holder_ref),
            (position_hbm, position_ref),
            (table_hbm, table_ref),
            (lengths_hbm, lengths_ref),
            (hidden_hbm, hidden_ref),
        ],
        sems,
    )
    for copy in copies[:4]:
        copy.wait()
    maps = slot_maps(holder_ref[...], peers)
    rows = hidden_ref.shape[0]
    place = (iota((HEAD, rows), 0) == position_ref[...]).astype(BF16)
    lane = iota((peers, HEAD), 1)
    depth = iota((peers, rows), 0) & (DEPTH - 1)
    length = jnp.zeros((peers, HEAD), F32)
    for step in range(PLANES):
        moved = moved_from(table_ref[...], source_at(depth, step))
        total = jnp.sum(jnp.where(moved, lengths_ref[...], 0).astype(F32), axis=1, keepdims=True)
        length = jnp.where(lane >= RANK * (step + 1), total, length)
    for c in range(2):
        out_ref[:, c, features:] = jnp.where(lane < RANK, nt(maps[c], place), length).astype(BF16)
    copies[4].wait()
    hidden = hidden_ref[...]
    for c in range(2):
        out_ref[:, c, :features] = nn(maps[c], hidden).astype(BF16)


def down_kernel(got_ref, down_ref, two_ref, partial_ref, pick_ref, limit_ref):
    del two_ref
    peers, _, width = got_ref.shape
    features = width - HEAD
    many = down_ref.shape[0]
    first, second = got_ref[:, 0, :], got_ref[:, 1, :]
    got = jnp.concatenate([first[:, :features], second[:, :features]], axis=0)
    place = jnp.concatenate([first[:, features:], second[:, features:]], axis=0)
    spread = (lax.shift_right_arithmetic(iota((many, HEAD), 0), 4) == iota((many, HEAD), 1)).astype(BF16)
    pick = nt(spread, place)
    pick_ref[...] = pick.astype(BF16)
    near = got_ref[pl.ds(my_plane() * DEPTH, DEPTH), 0, features:].astype(F32)
    for step in range(PLANES):
        lane = RANK * (step + 1)
        limit_ref[:, step] = jnp.broadcast_to(near[:, lane:lane + 1][:, :, None], limit_ref.shape[:1] + limit_ref.shape[2:])
    projected = nt(down_ref[...], got) * pick
    partial = jnp.sum(projected.reshape(many // RANK, RANK, 2 * peers), axis=0)
    for t in range(partial_ref.shape[0]):
        partial_ref[t] = partial


def up_kernel(got_ref, pick_ref, up_ref, out_ref):
    peers = out_ref.shape[0]
    low = jnp.sum(got_ref[...], axis=0).astype(BF16)
    many = up_ref.shape[0]
    spread = jnp.concatenate([low] * (many // RANK), axis=0) * pick_ref[...]
    delta = (tn(spread, up_ref[...]) * SCALE).astype(BF16)
    for c in range(2):
        out_ref[:, c, :] = delta[c * peers:(c + 1) * peers, :]


def gather_kernel(list_ref, cache_ref, own_ref, one_ref, two_ref, three_ref):
    count = list_ref.shape[0]
    for step, page_ref in enumerate((own_ref, one_ref, two_ref, three_ref)):
        first = ((my_plane() + step) & (PLANES - 1)) * DEPTH

        def copy(z, carry, page_ref=page_ref, first=first):
            for k in range(count):
                at = pl.ds(pl.multiple_of((z * count + k) * PAGE, PAGE), PAGE)
                page_ref[at, :] = cache_ref[list_ref[k, first + z]]
            return carry

        lax.fori_loop(0, DEPTH, copy, 0, unroll=8)


def prepare_kernel(holder_ref, table_ref, base_ref, weight_ref, route_ref, start_ref, down_ref):
    down_ref[...] = weight_ref[...]
    owners = route_ref.shape[1]
    maps = slot_maps(holder_ref[...], owners)
    moved = moved_map(table_ref[...], owners).astype(BF16)
    route_ref[...] = nt(jnp.concatenate(maps, axis=0), moved).astype(BF16)
    start = nn(moved, base_ref[...])
    for h in range(start_ref.shape[1]):
        start_ref[:, h, :] = start[:, h * HEAD:(h + 1) * HEAD]


def query_kernel(got_ref, route_ref, start_ref, one_ref, three_ref, out_ref, wide_ref):
    del one_ref, three_ref
    got = jnp.concatenate([got_ref[:, 0, :], got_ref[:, 1, :]], axis=0)
    chosen = tn(route_ref[...], got)
    for h in range(wide_ref.shape[1]):
        wide_ref[:, h, :] = chosen[:, h * HEAD:(h + 1) * HEAD]
    out_ref[...] = (start_ref[...] + wide_ref[...]).reshape(out_ref.shape).astype(BF16)


def weighted(scores, live, values):
    scores = jnp.where(live, scores * (HEAD ** -0.5), NEG)
    top = jnp.max(scores, axis=1, keepdims=True)
    weights = jnp.exp(scores - top)
    total = jnp.sum(weights, axis=1, keepdims=True)
    return nn((weights / total).astype(BF16), values)


def local_kernel(
    table_ref, lengths_ref, got_ref, base_ref, holder_ref, row_ref, cache_ref, out_ref, wide_ref, mixed_ref
):
    rows, heads, _ = wide_ref.shape
    pages = table_ref.shape[0]
    span = pages * PAGE
    maps = jnp.concatenate(slot_maps(holder_ref[...], got_ref.shape[0]), axis=0)
    delta = tn(maps, jnp.concatenate([got_ref[:, 0, :], got_ref[:, 1, :]], axis=0))
    query = (base_ref[...].astype(F32) + delta).astype(BF16).astype(F32)
    for h in range(heads):
        wide_ref[:, h, :] = query[:, h * HEAD:(h + 1) * HEAD]
    batch = 4
    shape = (batch * heads, batch * span)
    row_of = lax.div(iota(shape, 0), heads)
    column_of = lax.div(iota(shape, 1), span)
    place = lax.rem(iota(shape, 1), span)
    own = row_of == column_of

    def step(b, carry):
        first = b * batch
        found = []
        limit = jnp.zeros(shape, jnp.int32)
        for i in range(batch):
            limit = jnp.where(row_of == i, lengths_ref[0, first + i], limit)
            for j in range(pages):
                found.append(cache_ref[jnp.minimum(table_ref[j, first + i], POOL - 1)])
        both = jnp.concatenate(found, axis=0)
        q = wide_ref[pl.ds(first, batch)].reshape(batch * heads, HEAD).astype(BF16)
        scores = nt(q, both[:, :HEAD])
        mixed = weighted(scores, own & (place < limit), both[:, HEAD:])
        mixed_ref[pl.ds(first, batch)] = mixed.reshape(batch, heads, HEAD)
        return carry

    lax.fori_loop(0, rows // batch, step, 0, unroll=4)
    stays = jnp.where(row_ref[0:1, :] < POOL, 1.0, 0.0)
    eye = iota((rows, rows), 0) == iota((rows, rows), 1)
    keep = jnp.sum(jnp.where(eye, stays, 0.0), axis=1, keepdims=True)
    for h in range(heads):
        out_ref[:, h * HEAD:(h + 1) * HEAD] = (mixed_ref[:, h, :] * keep).astype(BF16)


def moved_kernel(query_ref, own_ref, one_ref, two_ref, three_ref, limit_ref, out_ref, wide_ref):
    depth, planes, heads, _ = limit_ref.shape
    span = own_ref.shape[0] // depth
    batch = HEAD // span
    wide = batch * heads
    shape = (wide, batch * span)
    own = lax.div(iota(shape, 0), heads) == lax.div(iota(shape, 1), span)
    place = jnp.where(own, lax.rem(iota(shape, 1), span), span).astype(F32)
    query = query_ref[...].astype(F32)
    parts = [(d, z) for d in range(planes) for z in range(0, depth, batch)]
    handed = (own_ref, one_ref, two_ref, three_ref)
    pages = [handed[d][z * span:(z + batch) * span, :] for d, z in parts]
    queries = [
        query[z:z + batch, d * heads:(d + 1) * heads].reshape(wide, HEAD).astype(BF16) for d, z in parts
    ]
    scores = [nt(q, page[:, :HEAD]) for q, page in zip(queries, pages)]
    live = [place < limit_ref[z:z + batch, d].reshape(wide, HEAD) for d, z in parts]
    scores = [jnp.where(m, x * (HEAD ** -0.5), NEG) for m, x in zip(live, scores)]
    tops = [jnp.max(x, axis=1, keepdims=True) for x in scores]
    weights = [jnp.exp(x - top) for x, top in zip(scores, tops)]
    totals = [jnp.sum(x, axis=1, keepdims=True) for x in weights]
    weights = [(x / total).astype(BF16) for x, total in zip(weights, totals)]
    mixed = [nn(x, page[:, HEAD:]) for x, page in zip(weights, pages)]
    for (d, z), x in zip(parts, mixed):
        wide_ref[z:z + batch, d * heads:(d + 1) * heads] = x.reshape(batch, heads, HEAD)
    out_ref[...] = wide_ref[...].astype(BF16)


def final_kernel(got_ref, local_ref, table_ref, out_ref, wide_ref):
    peers, heads, _ = wide_ref.shape
    wide_ref[...] = got_ref[...].astype(F32).reshape(wide_ref.shape)
    moved = moved_map(table_ref[...], peers).astype(BF16)
    for h in range(heads):
        part = tn(moved, wide_ref[:, h, :].astype(BF16))
        at = slice(h * HEAD, (h + 1) * HEAD)
        out_ref[:, at] = (part + local_ref[:, at].astype(F32)).astype(BF16)


def call(kernel, out_shape, cost, spaces, scratch=(), limit=24):
    kinds = {"s": pltpu.SMEM, "v": pltpu.VMEM, "h": pltpu.HBM, "a": pl.ANY}
    return pl.pallas_call(
        kernel,
        out_shape=out_shape,
        in_specs=[pl.BlockSpec(memory_space=kinds[x]) for x in spaces],
        out_specs=jax.tree.map(lambda _: pl.BlockSpec(memory_space=pltpu.VMEM), out_shape),
        scratch_shapes=list(scratch),
        cost_estimate=pl.CostEstimate(flops=cost, bytes_accessed=cost // 100, transcendentals=0),
        compiler_params=pltpu.CompilerParams(vmem_limit_bytes=limit * 1024 * 1024),
    )


def exchange(x, axis="replica", groups=None):
    return lax.all_to_all(x, axis, split_axis=0, concat_axis=0, tiled=True, axis_index_groups=groups)


def along_depth(x):
    return exchange(x, groups=[[p * DEPTH + z for z in range(DEPTH)] for p in range(PLANES)])


def hand_on(x, step):
    pairs = [
        (p * DEPTH + z, (p + step) % PLANES * DEPTH + z) for p in range(PLANES) for z in range(DEPTH)
    ]
    return lax.ppermute(x, "replica", pairs)


def body(
    hidden,
    base_query,
    key_value_cache,
    adapter_down_weight,
    adapter_up_weight,
    adapter_holder,
    adapter_position,
    request_page_table,
    lengths,
    migration_page_lists,
):
    rows, features = hidden.shape
    peers = lax.axis_size("replica")
    shards = lax.axis_size("tensor")
    heads = features // HEAD
    S = jax.ShapeDtypeStruct
    holder = adapter_holder.reshape(1, rows)
    position = adapter_position.reshape(1, rows)
    table = request_page_table.T
    length = lengths.reshape(1, rows)
    lists = migration_page_lists[0].T
    down = adapter_down_weight.reshape(-1, features)
    up = adapter_up_weight.reshape(-1, features)
    many = down.shape[0]

    ints = lambda n: pltpu.VMEM((n, rows), jnp.int32)
    sent = call(
        send_kernel,
        S((peers, 2, features + HEAD), BF16),
        10**8,
        "hhhhh",
        [pltpu.VMEM((rows, features), BF16), ints(1), ints(1), ints(table.shape[0]), ints(1), pltpu.SemaphoreType.DMA((5,))],
        limit=60,
    )(hidden, holder, position, table, length)
    got = exchange(sent)
    handed = S((DEPTH * lists.shape[0] * PAGE, 2 * HEAD), BF16)
    pages = call(gather_kernel, (handed,) * PLANES, 10**9, "sv")(lists, key_value_cache)
    route, start, down = call(
        prepare_kernel,
        (S((2 * peers, peers), BF16), S((peers, heads, HEAD), F32), S(down.shape, BF16)),
        10**8,
        "vvvv",
    )(holder, table, base_query, down)
    pages = [pages[0]] + [hand_on(pages[step], step) for step in range(1, PLANES)]

    partial, pick, limit = call(
        down_kernel,
        (S((shards, RANK, 2 * peers), F32), S((many, 2 * peers), BF16), S((DEPTH, PLANES, heads, HEAD), F32)),
        10**8,
        "vva",
    )(got, down, pages[2])
    partials = exchange(partial, "tensor")
    delta = call(up_kernel, S((peers, 2, features), BF16), 10**8, "vvv")(partials, pick, up)
    returned = exchange(delta)
    wide = pltpu.VMEM((rows, heads, HEAD), F32)
    flat = (DEPTH, PLANES * heads, HEAD)
    asked = along_depth(
        call(query_kernel, S(flat, BF16), 10**8, "vvvaa", (wide,))(returned, route, start, pages[1], pages[3])
    )
    local = call(local_kernel, S((rows, features), BF16), 10**9, "ssvvvvv", (wide, wide))(
        table, length, returned, base_query, holder, table, key_value_cache
    )
    answered = along_depth(
        call(moved_kernel, S(flat, BF16), 10**8, "vvvvvv", (pltpu.VMEM(flat, F32),))(asked, *pages, limit)
    )
    return call(final_kernel, S((rows, features), BF16), 10**8, "vvv", (wide,))(answered, local, table)


def solution(mesh):
    in_specs = (
        P("replica", "tensor"),
        P("replica", "tensor"),
        P("replica", None, "tensor"),
        P("replica", None, "tensor"),
        P("replica", None, "tensor"),
        P("replica", None),
        P("replica"),
        P("replica", None),
        P("replica"),
        P("replica", None, None),
    )
    return jax.shard_map(body, mesh=mesh, in_specs=in_specs, out_specs=P("replica", "tensor"), check_vma=False)
```
